512 devices in a mesh: ctx: 64 (over y, z), head: 8 (over x, core).
Axes of the slice: x: 4, y: 8, z: 8, core: 2. Of those that a mesh axis runs over, the one named last changes fastest.
Arguments:
- qkv_raw: bfloat16 [8192, 3, 2048], P('ctx', None, 'head'), may hold values from -6 to 6
- positions: int32 [8192], P('ctx'), may hold values from 0 to 8191, as said below
- filter_taps: float32 [3, 3, 2048], P(None, None, 'head'), may hold values from -1.2 to 1.2
- grad_out: bfloat16 [8192, 2048], P(('ctx', 'head')), may hold values from -6 to 6
Outputs:
- attn_out: bfloat16 [8192, 2048], P('ctx', 'head')
- qkv_grad: bfloat16 [8192, 3, 2048], P('ctx', None, 'head')
The draws below stay inside these ranges and needn't reach their ends.
Inputs may be any that keep to these rules, and one draw needn't show every extreme that they name: Rows 128 d to 128 d + 127 hold, in increasing order, the positions of group c and then those of group 2 * 64 - 1 - c, each group being 64 consecutive positions, where c = (d + r) mod 64 with one r for the whole array; every position appears once.
All inputs are finite; a program needn't handle non-finite values.
Results may differ from the reference program's by a relative error of at most 0.03.
Values may be sent and summed in bfloat16 or wider, within the bound.
A program may use at most 64 MiB of HBM per device.

```python
import math
import jax
import jax.numpy as jnp
from jax import lax

TOK_DEV = 128
HEAD_SIZE = 128
TAPS = 3
SEQ = 8192
CHANNELS = 2048
N_CTX = 64


def layout_rotation(key):
    return jax.random.randint(jax.random.fold_in(key, 101), (), 0, N_CTX)


def position_table(key):
    rotation = layout_rotation(key)
    group_len = TOK_DEV // 2
    row_ids = jnp.arange(SEQ, dtype=jnp.int32)
    device_ids = row_ids // TOK_DEV
    within = row_ids % TOK_DEV
    pair_ids = (device_ids + rotation) % N_CTX
    group_ids = jnp.where(within < group_len, pair_ids, 2 * N_CTX - 1 - pair_ids)
    return group_ids * group_len + within % group_len


def draw_positions(key, part):
    return position_table(key).astype(jnp.int32)


def draw_qkv_raw(key, part):
    base_key = jax.random.fold_in(key, 202)
    shape_all = (SEQ, 3, CHANNELS)
    values = jnp.clip(1.8 * jax.random.normal(base_key, shape_all, jnp.float32), -6.0, 6.0)
    return values.astype(jnp.bfloat16)


def draw_filter_taps(key, part):
    tap_key = jax.random.fold_in(key, 404)
    current = jax.random.uniform(jax.random.fold_in(tap_key, 1), (3, 1, CHANNELS), jnp.float32, 0.8, 1.0)
    earlier = jnp.clip(0.4 * jax.random.normal(jax.random.fold_in(tap_key, 2), (3, TAPS - 1, CHANNELS), jnp.float32), -1.2, 1.2)
    return jnp.concatenate([current, earlier], axis=1)


def steps_of(own_key, dims, shards, low, high):
    loudness, own = 1.0, jax.random.fold_in(own_key, 6)
    for axis_at, parts in shards:
        draws = jnp.exp(jax.random.uniform(jax.random.fold_in(own, axis_at), (parts,), jnp.float32, low / len(shards), high / len(shards)))
        loudness = loudness * jnp.repeat(draws, dims[axis_at] // parts).reshape([-1 if axis == axis_at else 1 for axis in range(len(dims))])
    return loudness


def scatter_about(key, shape, scale, limit, shards=(), kind=jnp.bfloat16):
    gain = steps_of(key, shape, shards, -0.22, 0.18) if shards else 1.0
    values = jax.random.normal(key, shape, jnp.float32) * scale * gain
    return jnp.minimum(jnp.maximum(values, -limit), limit).astype(kind)


def setup_inputs(seed: int = 0) -> dict:
    keys = jax.random.split(jax.random.key(seed), 5)
    return {
        "qkv_raw": draw_qkv_raw(jax.random.fold_in(keys[4], 71), 0),
        "positions": draw_positions(jax.random.fold_in(keys[4], 71), 0),
        "filter_taps": draw_filter_taps(jax.random.fold_in(keys[4], 71), 0),
        "grad_out": scatter_about(keys[3], (SEQ, CHANNELS), 1.0, 6.0, ((0, 512),)),
    }


NEG_LARGE = -1e+30

def featurize_full(raw_rows, filter_taps):
    seq_len = raw_rows.shape[0]
    padded = jnp.pad(raw_rows.astype(jnp.float32), ((TAPS - 1, 0), (0, 0), (0, 0)))
    result = jnp.zeros(raw_rows.shape, jnp.float32)
    for tap_index in range(TAPS):
        begin = TAPS - 1 - tap_index
        result = result + filter_taps[None, :, tap_index, :] * padded[begin:begin + seq_len]
    return result

def unfeaturize_full(grad_rows, filter_taps):
    seq_len = grad_rows.shape[0]
    padded = jnp.pad(grad_rows, ((0, TAPS - 1), (0, 0), (0, 0)))
    result = jnp.zeros(grad_rows.shape, jnp.float32)
    for tap_index in range(TAPS):
        result = result + filter_taps[None, :, tap_index, :] * padded[tap_index:tap_index + seq_len]
    return result

def forward_head(operands):
    query_rows, key_rows, value_rows, grad_rows = operands
    seq_len = query_rows.shape[0]
    block_rows = math.gcd(seq_len, 512)
    scaling = 1.0 / math.sqrt(query_rows.shape[1])
    key_wide = key_rows.astype(jnp.float32)
    col_ids = jnp.arange(seq_len, dtype=jnp.int32)

    def one_block(block_index):
        first_row = (block_index * block_rows).astype(jnp.int32)
        query_block = lax.dynamic_slice_in_dim(query_rows, first_row, block_rows, 0)
        grad_block = lax.dynamic_slice_in_dim(grad_rows, first_row, block_rows, 0)
        row_ids = first_row + jnp.arange(block_rows, dtype=jnp.int32)
        allowed = col_ids[None, :] <= row_ids[:, None]
        scores = jnp.dot(query_block, key_rows.T, preferred_element_type=jnp.float32) * scaling
        masked = jnp.where(allowed, scores, NEG_LARGE)
        top_score = lax.optimization_barrier(jnp.max(masked, axis=1, keepdims=True))
        summed = lax.optimization_barrier(jnp.sum(jnp.where(allowed, jnp.exp(masked - top_score), 0.0), axis=1))
        log_total = top_score[:, 0] + jnp.log(summed)
        probs = jnp.where(allowed, jnp.exp(masked - log_total[:, None]), 0.0)
        attn = jnp.dot(probs.astype(jnp.bfloat16), value_rows, preferred_element_type=jnp.float32).astype(jnp.bfloat16)
        delta = lax.optimization_barrier(jnp.sum(grad_block.astype(jnp.float32) * attn.astype(jnp.float32), axis=1))
        slopes = jnp.dot(grad_block, value_rows.T, preferred_element_type=jnp.float32)
        weighted = jnp.dot(probs * slopes, key_wide, precision=lax.Precision.HIGHEST)
        plain_sum = jnp.dot(probs, key_wide, precision=lax.Precision.HIGHEST)
        query_grad = scaling * (weighted - delta[:, None] * plain_sum)
        return (attn, log_total, delta, query_grad)
    results = lax.map(one_block, jnp.arange(seq_len // block_rows, dtype=jnp.int32))
    return tuple((stacked.reshape((seq_len,) + stacked.shape[2:]) for stacked in results))

def backward_head(operands):
    query_rows, key_rows, value_rows, grad_rows, log_total, delta = operands
    seq_len = query_rows.shape[0]
    block_rows = math.gcd(seq_len, 512)
    scaling = 1.0 / math.sqrt(query_rows.shape[1])
    row_ids = jnp.arange(seq_len, dtype=jnp.int32)

    def one_block(block_index):
        first_row = (block_index * block_rows).astype(jnp.int32)
        key_block = lax.dynamic_slice_in_dim(key_rows, first_row, block_rows, 0)
        value_block = lax.dynamic_slice_in_dim(value_rows, first_row, block_rows, 0)
        col_ids = first_row + jnp.arange(block_rows, dtype=jnp.int32)
        allowed = col_ids[None, :] <= row_ids[:, None]
        scores = jnp.dot(query_rows, key_block.T, preferred_element_type=jnp.float32) * scaling
        probs = jnp.where(allowed, jnp.exp(jnp.where(allowed, scores - log_total[:, None], NEG_LARGE)), 0.0)
        value_grad = jnp.dot(probs.astype(jnp.bfloat16).T, grad_rows, preferred_element_type=jnp.float32)
        slopes = jnp.dot(grad_rows, value_block.T, preferred_element_type=jnp.float32)
        dscores = (probs * (slopes - delta[:, None])).astype(jnp.bfloat16)
        key_grad = scaling * jnp.dot(dscores.T, query_rows, preferred_element_type=jnp.float32)
        return (key_grad, value_grad)
    results = lax.map(one_block, jnp.arange(seq_len // block_rows, dtype=jnp.int32))
    return tuple((stacked.reshape((seq_len,) + stacked.shape[2:]) for stacked in results))

def reference(qkv_raw, positions, filter_taps, grad_out):
    seq_len = positions.shape[0]
    heads_all = qkv_raw.shape[2] // HEAD_SIZE
    order = jnp.zeros((seq_len,), jnp.int32).at[positions].set(jnp.arange(seq_len, dtype=jnp.int32))
    raw_rows = qkv_raw[order]
    grad_rows = grad_out[order]
    featured = featurize_full(raw_rows, filter_taps).astype(jnp.bfloat16)

    def by_heads(matrix):
        return matrix.reshape(seq_len, heads_all, HEAD_SIZE).transpose(1, 0, 2)

    def from_heads(stacked):
        return stacked.transpose(1, 0, 2).reshape(seq_len, heads_all * HEAD_SIZE)
    query_heads = by_heads(featured[:, 0])
    key_heads = by_heads(featured[:, 1])
    value_heads = by_heads(featured[:, 2])
    grad_heads = by_heads(grad_rows)
    attn, log_total, delta, query_grad = lax.map(forward_head, (query_heads, key_heads, value_heads, grad_heads))
    key_grad, value_grad = lax.map(backward_head, (query_heads, key_heads, value_heads, grad_heads, log_total, delta))
    attn_rows = from_heads(attn)
    post_grads = jnp.stack([from_heads(query_grad), from_heads(key_grad), from_heads(value_grad)], axis=1)
    raw_grads = unfeaturize_full(post_grads, filter_taps)
    return (attn_rows[positions], raw_grads[positions].astype(jnp.bfloat16))
```

```python
import functools
import math

import jax
import jax.numpy as jnp
from jax import lax
from jax.experimental import pallas as pl
from jax.experimental.pallas import tpu as pltpu
from jax.sharding import PartitionSpec as P

HD = 128
MESH = pl.DeviceIdType.MESH
NEG = -1e30
F32 = jnp.float32
BF16 = jnp.bfloat16


def kernel(
    dims,
    raw_ref,
    pos_ref,
    taps_ref,
    gout_ref,
    attn_ref,
    grad_ref,
    land,
    halo_raw,
    q_all,
    d_all,
    k_all,
    v_all,
    k_code,
    w_all,
    s_all,
    p_low,
    x_low,
    stats,
    row_fac,
    row_del,
    part_o,
    part_q,
    part_k,
    part_v,
    rs_out,
    rs_in,
    fin,
    halo_out,
    halo_in,
    own_sem,
    a2a_send,
    a2a_recv,
    hr_send,
    hr_recv,
    ag_send,
    ag_recv,
    st_send,
    st_recv,
    rs_send,
    rs_recv,
    hg_send,
    hg_recv,
):
    Y, Z, H, G, NH, T = dims
    N = Y * Z
    d = lax.axis_index("ctx")
    hd = lax.axis_index("head")
    y = d // Z
    z = d % Z
    scaling = 1.0 / math.sqrt(HD)
    cexp = scaling * math.log2(math.e)

    d_next = (d + 1) % N
    d_prev = (d + N - 1) % N
    z_dev = lambda i: y * Z + i
    y_dev = lambda i: i * Z + z

    barrier = pltpu.get_barrier_semaphore()
    greet = [(z_dev((z + j) % Z), hd) for j in range(1, Z)]
    greet += [(y_dev((y + 1) % Y), hd), (y_dev((y + Y - 1) % Y), hd)]
    greet += [(d_next, hd), (d_prev, hd)]
    greet += [(d, (hd + j) % H) for j in range(1, H)]
    for dev in greet:
        pl.semaphore_signal(barrier, inc=1, device_id=dev, device_id_type=MESH)
    pl.semaphore_wait(barrier, len(greet))

    def remote(src, dst, s_sem, r_sem, dev):
        return pltpu.make_async_remote_copy(
            src_ref=src, dst_ref=dst, send_sem=s_sem, recv_sem=r_sem, device_id=dev, device_id_type=MESH
        )

    tail_e = remote(
        raw_ref.at[:, pl.ds(G - 16, 16)], halo_raw.at[0], hr_send.at[0], hr_recv.at[0], (d_next, hd)
    )
    tail_l = remote(
        raw_ref.at[:, pl.ds(2 * G - 16, 16)], halo_raw.at[1], hr_send.at[1], hr_recv.at[1], (d_prev, hd)
    )
    tail_e.start()
    tail_l.start()
    RB = 2 * G // H
    CW = NH * HD

    def a2a(j):
        to = (hd + j) % H
        return remote(
            gout_ref.at[:, pl.ds(pl.multiple_of(to * CW, CW), CW)],
            land.at[pl.ds(pl.multiple_of(hd * RB, RB), RB)],
            a2a_send.at[j - 1],
            a2a_recv.at[j - 1],
            (d, to),
        )

    def a2a_in(j):
        frm = (hd + H - j) % H
        return remote(
            gout_ref.at[:, pl.ds(pl.multiple_of(hd * CW, CW), CW)],
            land.at[pl.ds(pl.multiple_of(frm * RB, RB), RB)],
            a2a_send.at[j - 1],
            a2a_recv.at[j - 1],
            (d, frm),
        )

    for j in range(1, H):
        a2a(j).start()
    own = pltpu.make_async_copy(
        gout_ref.at[:, pl.ds(pl.multiple_of(hd * CW, CW), CW)],
        land.at[pl.ds(pl.multiple_of(hd * RB, RB), RB)],
        own_sem,
    )
    own.start()

    pair = pos_ref[0] // G
    rot = (pair - d + N) % N
    nk = Y * G
    nq = Z * G
    C = min(256, nq)
    ik = lax.broadcasted_iota(jnp.int32, (nk, C), 0)
    pk = ((ik // G) * Z + (z + rot)) % N
    k_code[0] = pk * G + ik % G
    k_code[1] = ik % G - pk * G

    def q_code(half, c):
        iq = lax.broadcasted_iota(jnp.int32, (1, C), 1) + c * C
        pq = (iq // G + (y * Z + rot)) % N
        return pq * G + iq % G if half == 0 else iq % G - pq * G

    rings = [
        (q_all, Z, z, z_dev, 0),
        (d_all, Z, z, z_dev, 1),
        (k_all, Y, y, y_dev, 0),
        (v_all, Y, y, y_dev, 1),
    ]

    def steps_of(n, flip):
        a, b = n // 2, n - 1 - n // 2
        return (b, a) if flip else (a, b)

    MR = max(Y, Z) // 2

    def ag_copy(h, item, way, s):
        buf, n, me, dev_of, flip = rings[item]
        sign = 1 if way == 0 else n - 1
        slot = (me + (n - sign) * s) % n
        dev = (dev_of((me + sign) % n), hd)
        return remote(
            buf.at[h, :, slot], buf.at[h, :, slot], ag_send.at[h, item, way, s], ag_recv.at[h, item, way, s], dev
        )

    def ag_wait(h, item, way, s):
        buf, n, me, dev_of, flip = rings[item]
        sign = 1 if way == 0 else n - 1
        slot = (me + (n - sign) * (s + 1)) % n
        dev = (dev_of((me + sign) % n), hd)
        remote(
            buf.at[h, :, slot], buf.at[h, :, slot], ag_send.at[h, item, way, s], ag_recv.at[h, item, way, s], dev
        ).wait_recv()

    def ag_round(h, s, items=(2, 0, 3, 1)):
        for item in items:
            n, flip = rings[item][1], rings[item][4]
            steps = steps_of(n, flip)
            for way in range(2):
                if 0 < s <= steps[way]:
                    ag_wait(h, item, way, s - 1)
                if s < steps[way]:
                    ag_copy(h, item, way, s).start()

    tail_e.wait_recv()
    tail_l.wait_recv()
    row = lax.broadcasted_iota(jnp.int32, (G, CW), 0)
    zero_rows = jnp.zeros((16, CW), F32)

    def featurize(kind, half):
        x = raw_ref[kind, pl.ds(half * G, G)].astype(F32)
        if half == 0:
            prior = jnp.where(pair == 0, zero_rows, halo_raw[0, kind].astype(F32))
        else:
            prior = jnp.where(
                pair == N - 1, raw_ref[kind, pl.ds(G - 16, 16)].astype(F32), halo_raw[1, kind].astype(F32)
            )
        tap = taps_ref[kind]
        out = tap[0:1] * x
        for t in range(1, T):
            moved = pltpu.roll(x, t, 0)
            for i in range(t):
                moved = jnp.where(row == i, prior[16 - t + i : 17 - t + i], moved)
            out = out + tap[t : t + 1] * moved
        return out.astype(BF16)

    for kind, buf, slot in ((1, k_all, y), (0, q_all, z), (2, v_all, y)):
        for half in range(2):
            out = featurize(kind, half)
            for h in range(NH):
                buf[h, half, slot] = out[:, h * HD : (h + 1) * HD]
        ag_round(0, 0, ((1, 2), (0, 0), (2, 3))[(1, 0, 2).index(kind)][1:])
    own.wait()
    for j in range(1, H):
        a2a_in(j).wait_recv()
    for half in range(2):
        for h in range(NH):
            d_all[h, half, z] = land[pl.ds(half * G, G), h * HD : (h + 1) * HD]
    ag_round(0, 0, (1,))

    NT = (((1,), (1,)), ((), ()))
    TN = (((0,), (0,)), ((), ()))
    NN = (((1,), (0,)), ((), ()))

    def mm(a, b, how):
        return lax.dot_general(a, b, how, preferred_element_type=F32)

    zc = C // G
    lanes = C // 128

    def pass1(h, half, c):
        q = q_all[h, half, pl.ds(c * zc, zc)].reshape(C, HD)
        g = d_all[h, half, pl.ds(c * zc, zc)].reshape(C, HD)
        cols = pl.ds(half * nq + c * C, C)
        tops = []
        score = []
        for kh in range(half + 1):
            keys = k_all[h, kh].reshape(nk, HD)
            sc = mm(keys, q, NT)
            if kh == half:
                sc = jnp.where(k_code[half] <= q_code(half, c), sc, NEG)
            score.append(sc)
            tops.append(jnp.max(sc, axis=0, keepdims=True))
        top = tops[0] if half == 0 else jnp.maximum(tops[0], tops[1])
        total = jnp.zeros((1, C), F32)
        tilt = jnp.zeros((1, C), F32)
        for kh in range(half + 1):
            w = jnp.exp2((score[kh] - top) * cexp)
            w_all[h, pl.ds(kh * nk, nk), cols] = w
            slope = mm(v_all[h, kh].reshape(nk, HD), g, NT)
            s_all[h, pl.ds(kh * nk, nk), cols] = slope
            total = total + jnp.sum(w, axis=0, keepdims=True)
            tilt = tilt + jnp.sum(w * slope, axis=0, keepdims=True)
        for i in range(lanes):
            r = (half * nq + c * C) // 128 + i
            for what, val in enumerate((top, total, tilt)):
                stats[h, z, what, pl.ds(r, 1)] = val[:, i * 128 : (i + 1) * 128]

    def st_copy(h, j, incoming=False):
        slot = (z + Z - j) % Z if incoming else z
        dev = z_dev((z + Z - j) % Z if incoming else (z + j) % Z)
        return remote(stats.at[h, slot], stats.at[h, slot], st_send.at[h, j - 1], st_recv.at[h, j - 1], (dev, hd))

    def st_start(h):
        for j in range(1, Z):
            st_copy(h, j).start()

    def st_finish(h):
        for j in range(1, Z):
            st_copy(h, j, True).wait_recv()
        top = stats[h, 0, 0]
        for i in range(1, Z):
            top = jnp.maximum(top, stats[h, i, 0])
        total = jnp.zeros_like(top)
        tilt = jnp.zeros_like(top)
        for i in range(Z):
            e = jnp.exp2((stats[h, i, 0] - top) * cexp)
            total = total + stats[h, i, 1] * e
            tilt = tilt + stats[h, i, 2] * e
        inv = 1.0 / total
        row_fac[h] = jnp.exp2((stats[h, z, 0] - top) * cexp) * inv
        row_del[h] = tilt * inv

    nr = 2 * nq // 128

    def row_of(ref, h, a, b):
        return jnp.concatenate([ref[h, pl.ds(i, 1)] for i in range(a // 128, b // 128)], axis=1)

    KC = min(256, nk)
    kz = KC // G

    def pass2_keys(h, kh, c):
        rows = pl.ds(kh * nk + c * KC, KC)
        lo = 0 if kh == 0 else nq
        cols = pl.ds(lo, 2 * nq - lo)
        fac = row_of(row_fac, h, lo, 2 * nq)
        dl = row_of(row_del, h, lo, 2 * nq)
        p = w_all[h, rows, cols] * fac
        pb = p.astype(BF16)
        p_low[rows, cols] = pb
        xb = (p * (s_all[h, rows, cols] - dl)).astype(BF16)
        x_low[rows, cols] = xb
        if kh == 0:
            g = d_all[h].reshape(2 * nq, HD)
            q = q_all[h].reshape(2 * nq, HD)
        else:
            g = d_all[h, 1].reshape(nq, HD)
            q = q_all[h, 1].reshape(nq, HD)
        part_v[h, kh, pl.ds(c * kz, kz)] = mm(pb, g, NN).reshape(kz, G, HD)
        part_k[h, kh, pl.ds(c * kz, kz)] = (mm(xb, q, NN) * scaling).reshape(kz, G, HD)

    def pass2_queries(h, half):
        ks = pl.ds(0, nk * (half + 1))
        cols = pl.ds(half * nq, nq)
        if half == 0:
            k = k_all[h, 0].reshape(nk, HD)
            v = v_all[h, 0].reshape(nk, HD)
        else:
            k = k_all[h].reshape(2 * nk, HD)
            v = v_all[h].reshape(2 * nk, HD)
        part_o[h, half] = mm(p_low[ks, cols], v, TN).reshape(Z, G, HD)
        part_q[h, half] = (mm(x_low[ks, cols], k, TN) * scaling).reshape(Z, G, HD)

    rs_rings = [
        (part_o, Z, z, z_dev, 0),
        (part_q, Z, z, z_dev, 1),
        (part_k, Y, y, y_dev, 0),
        (part_v, Y, y, y_dev, 1),
    ]

    def rs_copy(h, item, way, s):
        part, n, me, dev_of, flip = rs_rings[item]
        sign = 1 if way == 0 else n - 1
        return remote(
            rs_out.at[h, item, way, s],
            rs_in.at[h, item, way, s],
            rs_send.at[h, item, way, s],
            rs_recv.at[h, item, way, s],
            (dev_of((me + sign) % n), hd),
        )

    def rs_round(h, s, items=(2, 0, 3, 1)):
        for item in items:
            part, n, me, dev_of, flip = rs_rings[item]
            steps = steps_of(n, flip)
            for way in range(2):
                count = steps[way]
                if s < count:
                    sign = 1 if way == 0 else n - 1
                    dest = (me + sign * (count - s)) % n
                    val = part[h, :, pl.ds(dest, 1)].reshape(2, G, HD)
                    if s > 0:
                        rs_copy(h, item, way, s - 1).wait_recv()
                        val = val + rs_in[h, item, way, s - 1].astype(F32)
                    rs_out[h, item, way, s] = val.astype(BF16)
                    rs_copy(h, item, way, s).start()

    def rs_final(h, item):
        part, n, me, dev_of, flip = rs_rings[item]
        steps = steps_of(n, flip)
        val = part[h, :, pl.ds(me, 1)].reshape(2, G, HD)
        for way in range(2):
            if steps[way] > 0:
                rs_copy(h, item, way, steps[way] - 1).wait_recv()
                val = val + rs_in[h, item, way, steps[way] - 1].astype(F32)
        return val

    def hg_copy(h, half):
        return remote(
            halo_out.at[h, half],
            halo_in.at[h, half],
            hg_send.at[h, half],
            hg_recv.at[h, half],
            (d_prev if half == 0 else d_next, hd),
        )

    def finish_sums(h):
        for kind, item in ((0, 1), (1, 2), (2, 3)):
            val = rs_final(h, item)
            fin[h, kind] = val
            for half in range(2):
                halo_out[h, half, kind] = val[half, 0:8]
        for half in range(2):
            hg_copy(h, half).start()
        o = rs_final(h, 0).astype(BF16)
        for half in range(2):
            attn_ref[pl.ds(half * G, G), h * HD : (h + 1) * HD] = o[half]

    row1 = lax.broadcasted_iota(jnp.int32, (G, HD), 0)

    def finish_grads(h):
        for half in range(2):
            hg_copy(h, half).wait_recv()
        for kind in range(3):
            tap = taps_ref[kind][:, h * HD : (h + 1) * HD]
            for half in range(2):
                x = fin[h, kind, half]
                if half == 0:
                    nxt = jnp.where(pair == N - 1, fin[h, kind, 1, 0:8], halo_in[h, 0, kind])
                else:
                    nxt = jnp.where(pair == 0, jnp.zeros((8, HD), F32), halo_in[h, 1, kind])
                out = tap[0:1] * x
                for t in range(1, T):
                    moved = pltpu.roll(x, G - t, 0)
                    for i in range(t):
                        moved = jnp.where(row1 == G - t + i, nxt[i : i + 1], moved)
                    out = out + tap[t : t + 1] * moved
                grad_ref[kind, pl.ds(half * G, G), h * HD : (h + 1) * HD] = out.astype(BF16)

    nc = nq // C
    kc = nk // KC
    chunks = [(1, c) for c in range(nc)] + [(0, c) for c in range(nc)]
    for s in range(1, MR + 1):
        if s == min(3, MR):
            ag_round(1, 0)
        ag_round(0, s)
    done = 1
    for half, c in chunks:
        if done < MR:
            ag_round(1, done)
            done += 1
        pass1(0, half, c)
    while done <= MR:
        ag_round(1, done)
        done += 1
    st_start(0)
    for half, c in chunks:
        pass1(1, half, c)
    st_start(1)
    st_finish(0)
    for kh in range(2):
        for c in range(kc):
            pass2_keys(0, kh, c)
    rs_round(0, 0, (2, 3))
    for half in range(2):
        pass2_queries(0, half)
    rs_round(0, 0, (0, 1))
    st_finish(1)
    done = 1
    for kh in range(2):
        for c in range(kc):
            pass2_keys(1, kh, c)
            if done < MR:
                rs_round(0, done)
                done += 1
    rs_round(1, 0, (2, 3))
    for half in range(2):
        pass2_queries(1, half)
    rs_round(1, 0, (0, 1))
    while done < MR:
        rs_round(0, done)
        done += 1
    finish_sums(0)
    for s in range(1, MR):
        rs_round(1, s)
    finish_sums(1)
    finish_grads(0)
    finish_grads(1)

    tail_e.wait_send()
    tail_l.wait_send()
    for j in range(1, H):
        a2a(j).wait_send()
    for h in range(NH):
        for item in range(4):
            n, flip = rings[item][1], rings[item][4]
            steps = steps_of(n, flip)
            for way in range(2):
                for s in range(steps[way]):
                    ag_copy(h, item, way, s).wait_send()
                    rs_copy(h, item, way, s).wait_send()
        for j in range(1, Z):
            st_copy(h, j).wait_send()
        for half in range(2):
            hg_copy(h, half).wait_send()


def local(Y, Z, H, qkv_raw, positions, filter_taps, grad_out):
    rows = positions.shape[0]
    G = rows // 2
    CW = qkv_raw.shape[2]
    NH = CW // HD
    T = filter_taps.shape[1]
    MR = max(Y, Z) // 2
    nq, nk = Z * G, Y * G
    C = min(256, nq)
    nr = 2 * nq // 128
    raw = jnp.transpose(qkv_raw, (1, 0, 2))
    dma = pltpu.SemaphoreType.DMA
    vmem = pl.BlockSpec(memory_space=pltpu.VMEM)
    attn, grad = pl.pallas_call(
        functools.partial(kernel, (Y, Z, H, G, NH, T)),
        out_shape=(
            jax.ShapeDtypeStruct((rows, CW), BF16),
            jax.ShapeDtypeStruct((3, rows, CW), BF16),
        ),
        in_specs=[vmem, pl.BlockSpec(memory_space=pltpu.SMEM), vmem, vmem],
        out_specs=(vmem, vmem),
        scratch_shapes=[
            pltpu.VMEM((rows, CW), BF16),
            pltpu.VMEM((2, 3, 16, CW), BF16),
            pltpu.VMEM((NH, 2, Z, G, HD), BF16),
            pltpu.VMEM((NH, 2, Z, G, HD), BF16),
            pltpu.VMEM((NH, 2, Y, G, HD), BF16),
            pltpu.VMEM((NH, 2, Y, G, HD), BF16),
            pltpu.VMEM((2, nk, C), jnp.int32),
            pltpu.VMEM((NH, 2 * nk, 2 * nq), F32),
            pltpu.VMEM((NH, 2 * nk, 2 * nq), F32),
            pltpu.VMEM((2 * nk, 2 * nq), BF16),
            pltpu.VMEM((2 * nk, 2 * nq), BF16),
            pltpu.VMEM((NH, Z, 3, nr, 128), F32),
            pltpu.VMEM((NH, nr, 128), F32),
            pltpu.VMEM((NH, nr, 128), F32),
            pltpu.VMEM((NH, 2, Z, G, HD), F32),
            pltpu.VMEM((NH, 2, Z, G, HD), F32),
            pltpu.VMEM((NH, 2, Y, G, HD), F32),
            pltpu.VMEM((NH, 2, Y, G, HD), F32),
            pltpu.VMEM((NH, 4, 2, MR, 2, G, HD), BF16),
            pltpu.VMEM((NH, 4, 2, MR, 2, G, HD), BF16),
            pltpu.VMEM((NH, 3, 2, G, HD), F32),
            pltpu.VMEM((NH, 2, 3, 8, HD), F32),
            pltpu.VMEM((NH, 2, 3, 8, HD), F32),
            dma,
            dma((H - 1,)),
            dma((H - 1,)),
            dma((2,)),
            dma((2,)),
            dma((NH, 4, 2, MR)),
            dma((NH, 4, 2, MR)),
            dma((NH, Z - 1)),
            dma((NH, Z - 1)),
            dma((NH, 4, 2, MR)),
            dma((NH, 4, 2, MR)),
            dma((NH, 2)),
            dma((NH, 2)),
        ],
        compiler_params=pltpu.CompilerParams(
            collective_id=0, has_side_effects=True, vmem_limit_bytes=56 * 1024 * 1024
        ),
    )(raw, positions, filter_taps, grad_out)
    return attn, jnp.transpose(grad, (1, 0, 2))


def solution(mesh):
    n = mesh.shape["ctx"]
    Y = 1
    while (2 * Y) * (2 * Y) <= n and n % (2 * Y) == 0:
        Y *= 2
    in_specs = (P("ctx", None, "head"), P("ctx"), P(None, None, "head"), P(("ctx", "head"), None))
    out_specs = (P("ctx", "head"), P("ctx", None, "head"))
    return jax.shard_map(
        functools.partial(local, Y, n // Y, mesh.shape["head"]),
        mesh=mesh,
        in_specs=in_specs,
        out_specs=out_specs,
        check_vma=False,
    )
```

```python
import functools
import math

import jax
import jax.numpy as jnp
from jax import lax
from jax.experimental import pallas as pl
from jax.experimental.pallas import tpu as pltpu
from jax.sharding import PartitionSpec as P

HD = 128
MESH = pl.DeviceIdType.MESH
NEG = -1e30
F32 = jnp.float32
BF16 = jnp.bfloat16


def kernel(
    dims,
    raw_ref,
    pos_ref,
    taps_ref,
    gout_ref,
    attn_ref,
    grad_ref,
    land,
    halo_raw,
    q_all,
    d_all,
    kv_all,
    k_code,
    w_all,
    s_all,
    p_low,
    x_low,
    stats,
    row_fac,
    row_del,
    part_o,
    part_q,
    part_k,
    part_v,
    rs_out,
    rs_in,
    fin,
    halo_out,
    halo_in,
    own_sem,
    a2a_send,
    a2a_recv,
    hr_send,
    hr_recv,
    ag_send,
    ag_recv,
    st_send,
    st_recv,
    rs_send,
    rs_recv,
    hg_send,
    hg_recv,
):
    Y, Z, H, G, NH, T = dims
    N = Y * Z
    d = lax.axis_index("ctx")
    hd = lax.axis_index("head")
    y = d // Z
    z = d % Z
    scaling = 1.0 / math.sqrt(HD)
    cexp = scaling * math.log2(math.e)

    d_next = (d + 1) % N
    d_prev = (d + N - 1) % N
    z_dev = lambda i: y * Z + i
    y_dev = lambda i: i * Z + z

    barrier = pltpu.get_barrier_semaphore()
    greet = [(z_dev((z + j) % Z), hd) for j in range(1, Z)]
    greet += [(y_dev((y + j) % Y), hd) for j in range(1, Y) if j <= 2 or Y - j <= 2]
    greet += [(d_next, hd), (d_prev, hd)]
    greet += [(d, (hd + j) % H) for j in range(1, H)]
    for dev in greet:
        pl.semaphore_signal(barrier, inc=1, device_id=dev, device_id_type=MESH)

    def remote(src, dst, s_sem, r_sem, dev):
        return pltpu.make_async_remote_copy(
            src_ref=src, dst_ref=dst, send_sem=s_sem, recv_sem=r_sem, device_id=dev, device_id_type=MESH
        )

    tail_e = remote(
        raw_ref.at[:, pl.ds(G - 16, 16)], halo_raw.at[0], hr_send.at[0], hr_recv.at[0], (d_next, hd)
    )
    tail_l = remote(
        raw_ref.at[:, pl.ds(2 * G - 16, 16)], halo_raw.at[1], hr_send.at[1], hr_recv.at[1], (d_prev, hd)
    )
    RB = 2 * G // H
    CW = NH * HD

    def a2a(j):
        to = (hd + j) % H
        return remote(
            gout_ref.at[:, pl.ds(pl.multiple_of(to * CW, CW), CW)],
            land.at[pl.ds(pl.multiple_of(hd * RB, RB), RB)],
            a2a_send.at[j - 1],
            a2a_recv.at[j - 1],
            (d, to),
        )

    def a2a_in(j):
        frm = (hd + H - j) % H
        return remote(
            gout_ref.at[:, pl.ds(pl.multiple_of(hd * CW, CW), CW)],
            land.at[pl.ds(pl.multiple_of(frm * RB, RB), RB)],
            a2a_send.at[j - 1],
            a2a_recv.at[j - 1],
            (d, frm),
        )

    own = pltpu.make_async_copy(
        gout_ref.at[:, pl.ds(pl.multiple_of(hd * CW, CW), CW)],
        land.at[pl.ds(pl.multiple_of(hd * RB, RB), RB)],
        own_sem,
    )
    own.start()

    pair = pos_ref[0] // G
    rot = (pair - d + N) % N
    nk = Y * G
    nq = Z * G
    C = min(256, nq)
    group_of = lambda i: i >> (G.bit_length() - 1)

    def wrap(p):
        p = jnp.where(p >= 2 * N, p - 2 * N, p)
        return jnp.where(p >= N, p - N, p)

    def q_code(half, c):
        iq = lax.broadcasted_iota(jnp.int32, (1, C), 1) + c * C
        pq = wrap(group_of(iq) + (y * Z + rot))
        return pq * G + (iq & (G - 1)) if half == 0 else (iq & (G - 1)) - pq * G

    E = 16
    gathers = []
    for h in range(NH):
        gathers += [
            (lambda i, h=h: kv_all.at[0, h, :, i, pl.ds(E, G - E)], Y, y, y_dev),
            (lambda i, h=h: q_all.at[h, :, i, pl.ds(E, G - E)], Z, z, z_dev),
            (lambda i, h=h: kv_all.at[1, h, :, i, pl.ds(E, G - E)], Y, y, y_dev),
            (lambda i, h=h: d_all.at[h, :, i], Z, z, z_dev),
        ]
    gathers += [
        (lambda i: kv_all.at[:, :, :, i, pl.ds(0, E)], Y, y, y_dev),
        (lambda i: q_all.at[:, :, i, pl.ds(0, E)], Z, z, z_dev),
    ]
    K_EDGE, Q_EDGE = 4 * NH, 4 * NH + 1
    flips = (0, 0, 1, 1) * NH + (1, 1)

    def steps_of(n, flip):
        a, b = n // 2, n - 1 - n // 2
        return (b, a) if flip else (a, b)

    def ag_copy(item, way, dist, incoming=False):
        view, n, me, dev_of = gathers[item]
        sign = 1 if way == 0 else n - 1
        hop = dist if dist <= 2 else dist - 2
        if incoming:
            slot = (me + (n - sign) * dist) % n
        else:
            slot = me if dist <= 2 else (me + (n - sign) * 2) % n
        dev = (dev_of((me + sign * hop) % n), hd)
        return remote(
            view(slot), view(slot), ag_send.at[item, way, dist - 1], ag_recv.at[item, way, dist - 1], dev
        )

    def ag_counts(item):
        return enumerate(steps_of(gathers[item][1], flips[item]))

    def ag_first(item):
        for dist in (2, 1):
            for way, count in ag_counts(item):
                if dist <= count:
                    ag_copy(item, way, dist).start()

    def ag_relay(item):
        for way, count in ag_counts(item):
            if count >= 2:
                ag_copy(item, way, 2, True).wait_recv()
            for dist in (4, 3):
                if dist <= count:
                    ag_copy(item, way, dist).start()

    def ag_last(item):
        for way, count in ag_counts(item):
            for dist in (1, 3, 4):
                if dist <= count:
                    ag_copy(item, way, dist, True).wait_recv()

    zero_rows = jnp.zeros((16, CW), F32)

    def featurize(kind, half, prior, rows):
        x = raw_ref[kind, pl.ds(half * G, rows)].astype(F32)
        row = lax.broadcasted_iota(jnp.int32, (rows, CW), 0)
        tap = taps_ref[kind]
        out = tap[0:1] * x
        for t in range(1, T):
            moved = pltpu.roll(x, t, 0)
            if prior is not None:
                for i in range(t):
                    moved = jnp.where(row == i, prior[16 - t + i : 17 - t + i], moved)
            out = out + tap[t : t + 1] * moved
        return out.astype(BF16)

    def own_view(kind, h, half):
        return q_all.at[h, half, z] if kind == 0 else kv_all.at[kind - 1, h, half, y]

    for kind in (1, 0, 2):
        for half in range(2):
            out = featurize(kind, half, None, G)
            for h in range(NH):
                own_view(kind, h, half)[pl.ds(E, G - E)] = out[E:, h * HD : (h + 1) * HD]

    pl.semaphore_wait(barrier, len(greet))
    tail_e.start()
    tail_l.start()
    for j in range(1, H):
        a2a(j).start()
    for h in range(NH):
        for item in range(3):
            ag_first(4 * h + item)

    tail_e.wait_recv()
    tail_l.wait_recv()
    for kind in range(3):
        for half in range(2):
            if half == 0:
                prior = jnp.where(pair == 0, zero_rows, halo_raw[0, kind].astype(F32))
            else:
                prior = jnp.where(
                    pair == N - 1, raw_ref[kind, pl.ds(G - 16, 16)].astype(F32), halo_raw[1, kind].astype(F32)
                )
            out = featurize(kind, half, prior, E)
            for h in range(NH):
                own_view(kind, h, half)[pl.ds(0, E)] = out[:, h * HD : (h + 1) * HD]
    ag_first(K_EDGE)
    ag_first(Q_EDGE)
    own.wait()
    for j in range(1, H):
        a2a_in(j).wait_recv()
    for half in range(2):
        for h in range(NH):
            d_all[h, half, z] = land[pl.ds(half * G, G), h * HD : (h + 1) * HD]
    for h in range(NH):
        ag_first(4 * h + 3)

    ik = lax.broadcasted_iota(jnp.int32, (nk, C), 0)
    pk = wrap(group_of(ik) * Z + (z + rot))
    k_code[0] = pk * G + (ik & (G - 1))
    k_code[1] = (ik & (G - 1)) - pk * G

    NT = (((1,), (1,)), ((), ()))
    TN = (((0,), (0,)), ((), ()))
    NN = (((1,), (0,)), ((), ()))

    def mm(a, b, how):
        return lax.dot_general(a, b, how, preferred_element_type=F32)

    zc = C // G
    lanes = C // 128

    def pass1(h, half, c):
        q = q_all[h, half, pl.ds(c * zc, zc)].reshape(C, HD)
        g = d_all[h, half, pl.ds(c * zc, zc)].reshape(C, HD)
        cols = pl.ds(half * nq + c * C, C)
        tops = []
        score = []
        for kh in range(half + 1):
            keys = kv_all[0, h, kh].reshape(nk, HD)
            sc = mm(keys, q, NT)
            if kh == half:
                sc = jnp.where(k_code[half] <= q_code(half, c), sc, NEG)
            score.append(sc)
            tops.append(jnp.max(sc, axis=0, keepdims=True))
        top = tops[0] if half == 0 else jnp.maximum(tops[0], tops[1])
        total = jnp.zeros((1, C), F32)
        tilt = jnp.zeros((1, C), F32)
        for kh in range(half + 1):
            w = jnp.exp2((score[kh] - top) * cexp)
            w_all[h, pl.ds(kh * nk, nk), cols] = w
            slope = mm(kv_all[1, h, kh].reshape(nk, HD), g, NT)
            s_all[h, pl.ds(kh * nk, nk), cols] = slope
            total = total + jnp.sum(w, axis=0, keepdims=True)
            tilt = tilt + jnp.sum(w * slope, axis=0, keepdims=True)
        for i in range(lanes):
            r = (half * nq + c * C) // 128 + i
            for what, val in enumerate((top, total, tilt)):
                stats[h, z, what, pl.ds(r, 1)] = val[:, i * 128 : (i + 1) * 128]

    def st_copy(h, j, incoming=False):
        slot = (z + Z - j) % Z if incoming else z
        dev = z_dev((z + Z - j) % Z if incoming else (z + j) % Z)
        return remote(stats.at[h, slot], stats.at[h, slot], st_send.at[h, j - 1], st_recv.at[h, j - 1], (dev, hd))

    def st_start(h):
        for j in range(1, Z):
            st_copy(h, j).start()

    def st_finish(h):
        for j in range(1, Z):
            st_copy(h, j, True).wait_recv()
        top = stats[h, 0, 0]
        for i in range(1, Z):
            top = jnp.maximum(top, stats[h, i, 0])
        total = jnp.zeros_like(top)
        tilt = jnp.zeros_like(top)
        for i in range(Z):
            e = jnp.exp2((stats[h, i, 0] - top) * cexp)
            total = total + stats[h, i, 1] * e
            tilt = tilt + stats[h, i, 2] * e
        inv = 1.0 / total
        row_fac[h] = jnp.exp2((stats[h, z, 0] - top) * cexp) * inv
        row_del[h] = tilt * inv

    nr = 2 * nq // 128

    def row_of(ref, h, a, b):
        return jnp.concatenate([ref[h, pl.ds(i, 1)] for i in range(a // 128, b // 128)], axis=1)

    KC = min(256, nk)
    kz = KC // G

    def pass2_keys(h, kh, c):
        rows = pl.ds(kh * nk + c * KC, KC)
        lo = 0 if kh == 0 else nq
        cols = pl.ds(lo, 2 * nq - lo)
        fac = row_of(row_fac, h, lo, 2 * nq)
        dl = row_of(row_del, h, lo, 2 * nq)
        p = w_all[h, rows, cols] * fac
        pb = p.astype(BF16)
        p_low[rows, cols] = pb
        xb = (p * (s_all[h, rows, cols] - dl)).astype(BF16)
        x_low[rows, cols] = xb
        if kh == 0:
            g = d_all[h].reshape(2 * nq, HD)
            q = q_all[h].reshape(2 * nq, HD)
        else:
            g = d_all[h, 1].reshape(nq, HD)
            q = q_all[h, 1].reshape(nq, HD)
        part_v[h, kh, pl.ds(c * kz, kz)] = mm(pb, g, NN).reshape(kz, G, HD)
        part_k[h, kh, pl.ds(c * kz, kz)] = (mm(xb, q, NN) * scaling).reshape(kz, G, HD)

    def pass2_queries(h, half):
        ks = pl.ds(0, nk * (half + 1))
        cols = pl.ds(half * nq, nq)
        if half == 0:
            k = kv_all[0, h, 0].reshape(nk, HD)
            v = kv_all[1, h, 0].reshape(nk, HD)
        else:
            k = kv_all[0, h].reshape(2 * nk, HD)
            v = kv_all[1, h].reshape(2 * nk, HD)
        part_o[h, half] = mm(p_low[ks, cols], v, TN).reshape(Z, G, HD)
        part_q[h, half] = (mm(x_low[ks, cols], k, TN) * scaling).reshape(Z, G, HD)

    rs_rings = [
        (part_o, Z, z, z_dev, 0),
        (part_q, Z, z, z_dev, 1),
        (part_k, Y, y, y_dev, 0),
        (part_v, Y, y, y_dev, 1),
    ]

    def rs_copy(h, item, way, dist):
        part, n, me, dev_of, flip = rs_rings[item]
        sign = 1 if way == 0 else n - 1
        hop = dist if dist <= 2 else dist - 2
        return remote(
            rs_out.at[h, item, way, dist - 1],
            rs_in.at[h, item, way, dist - 1],
            rs_send.at[h, item, way, dist - 1],
            rs_recv.at[h, item, way, dist - 1],
            (dev_of((me + sign * hop) % n), hd),
        )

    def rs_counts(item):
        return enumerate(steps_of(rs_rings[item][1], rs_rings[item][4]))

    def rs_put(h, item, way, dist):
        part, n, me, dev_of, flip = rs_rings[item]
        sign = 1 if way == 0 else n - 1
        val = part[h, :, pl.ds((me + sign * dist) % n, 1)].reshape(2, G, HD)
        if dist == 2:
            count = steps_of(n, flip)[way]
            for more in (3, 4):
                if more <= count:
                    rs_copy(h, item, way, more).wait_recv()
                    val = val + rs_in[h, item, way, more - 1].astype(F32)
        rs_out[h, item, way, dist - 1] = val.astype(BF16)
        rs_copy(h, item, way, dist).start()

    def rs_first(h, item):
        for dist in (4, 3, 1):
            for way, count in rs_counts(item):
                if dist <= count:
                    rs_put(h, item, way, dist)

    def rs_relay(h, item):
        for way, count in rs_counts(item):
            if count >= 2:
                rs_put(h, item, way, 2)

    def rs_final(h, item):
        part, n, me, dev_of, flip = rs_rings[item]
        val = part[h, :, pl.ds(me, 1)].reshape(2, G, HD)
        for way, count in rs_counts(item):
            for dist in (1, 2):
                if dist <= count:
                    rs_copy(h, item, way, dist).wait_recv()
                    val = val + rs_in[h, item, way, dist - 1].astype(F32)
        return val

    def hg_copy(h, half):
        return remote(
            halo_out.at[h, half],
            halo_in.at[h, half],
            hg_send.at[h, half],
            hg_recv.at[h, half],
            (d_prev if half == 0 else d_next, hd),
        )

    def finish_sums(h):
        for kind, item in ((0, 1), (1, 2), (2, 3)):
            val = rs_final(h, item)
            fin[h, kind] = val
            for half in range(2):
                halo_out[h, half, kind] = val[half, 0:8]
        for half in range(2):
            hg_copy(h, half).start()
        o = rs_final(h, 0).astype(BF16)
        for half in range(2):
            attn_ref[pl.ds(half * G, G), h * HD : (h + 1) * HD] = o[half]

    row1 = lax.broadcasted_iota(jnp.int32, (G, HD), 0)

    def finish_grads(h):
        for half in range(2):
            hg_copy(h, half).wait_recv()
        for kind in range(3):
            tap = taps_ref[kind][:, h * HD : (h + 1) * HD]
            for half in range(2):
                x = fin[h, kind, half]
                if half == 0:
                    nxt = jnp.where(pair == N - 1, fin[h, kind, 1, 0:8], halo_in[h, 0, kind])
                else:
                    nxt = jnp.where(pair == 0, jnp.zeros((8, HD), F32), halo_in[h, 1, kind])
                out = tap[0:1] * x
                for t in range(1, T):
                    moved = pltpu.roll(x, G - t, 0)
                    for i in range(t):
                        moved = jnp.where(row1 == G - t + i, nxt[i : i + 1], moved)
                    out = out + tap[t : t + 1] * moved
                grad_ref[kind, pl.ds(half * G, G), h * HD : (h + 1) * HD] = out.astype(BF16)

    nc = nq // C
    kc = nk // KC
    chunks = [(1, c) for c in range(nc)] + [(0, c) for c in range(nc)]
    for item in (0, 1, 2, 4, 5, 6, K_EDGE, Q_EDGE, 3):
        ag_relay(item)
    for item in (0, 1, 2, K_EDGE, Q_EDGE, 3):
        ag_last(item)
    for half, c in chunks[:nc]:
        pass1(0, half, c)
    ag_relay(7)
    for half, c in chunks[nc:]:
        pass1(0, half, c)
    st_start(0)
    for item in (4, 5, 6, 7):
        ag_last(item)
    for half, c in chunks:
        pass1(1, half, c)
    st_start(1)
    st_finish(0)
    for kh in range(2):
        for c in range(kc):
            pass2_keys(0, kh, c)
    rs_first(0, 2)
    rs_first(0, 3)
    for half in range(2):
        pass2_queries(0, half)
    rs_first(0, 1)
    rs_first(0, 0)
    st_finish(1)
    for kh in range(2):
        for c in range(kc):
            pass2_keys(1, kh, c)
    rs_first(1, 2)
    rs_first(1, 3)
    rs_relay(0, 2)
    rs_relay(0, 3)
    for half in range(2):
        pass2_queries(1, half)
    rs_first(1, 1)
    rs_first(1, 0)
    rs_relay(0, 1)
    rs_relay(0, 0)
    for item in (2, 3, 1, 0):
        rs_relay(1, item)
    finish_sums(0)
    finish_sums(1)
    finish_grads(0)
    finish_grads(1)

    tail_e.wait_send()
    tail_l.wait_send()
    for j in range(1, H):
        a2a(j).wait_send()
    for item in range(len(gathers)):
        for way, count in ag_counts(item):
            for dist in range(1, count + 1):
                ag_copy(item, way, dist).wait_send()
    for h in range(NH):
        for item in range(4):
            for way, count in rs_counts(item):
                for dist in range(1, count + 1):
                    rs_copy(h, item, way, dist).wait_send()
        for j in range(1, Z):
            st_copy(h, j).wait_send()
        for half in range(2):
            hg_copy(h, half).wait_send()


def hand_on(attn_in, grad_in, attn_out, grad_out):
    attn_out[...] = attn_in[...]
    grad_out[...] = grad_in[...]


def local(Y, Z, H, qkv_raw, positions, filter_taps, grad_out):
    rows = positions.shape[0]
    G = rows // 2
    CW = qkv_raw.shape[2]
    NH = CW // HD
    T = filter_taps.shape[1]
    MR = max(Y, Z) // 2
    nq, nk = Z * G, Y * G
    C = min(256, nq)
    nr = 2 * nq // 128
    raw = jnp.transpose(qkv_raw, (1, 0, 2))
    dma = pltpu.SemaphoreType.DMA
    vmem = pl.BlockSpec(memory_space=pltpu.VMEM)
    attn, grad = pl.pallas_call(
        functools.partial(kernel, (Y, Z, H, G, NH, T)),
        out_shape=(
            jax.ShapeDtypeStruct((rows, CW), BF16),
            jax.ShapeDtypeStruct((3, rows, CW), BF16),
        ),
        in_specs=[vmem, pl.BlockSpec(memory_space=pltpu.SMEM), vmem, vmem],
        out_specs=(vmem, vmem),
        scratch_shapes=[
            pltpu.VMEM((rows, CW), BF16),
            pltpu.VMEM((2, 3, 16, CW), BF16),
            pltpu.VMEM((NH, 2, Z, G, HD), BF16),
            pltpu.VMEM((NH, 2, Z, G, HD), BF16),
            pltpu.VMEM((2, NH, 2, Y, G, HD), BF16),
            pltpu.VMEM((2, nk, C), jnp.int32),
            pltpu.VMEM((NH, 2 * nk, 2 * nq), F32),
            pltpu.VMEM((NH, 2 * nk, 2 * nq), F32),
            pltpu.VMEM((2 * nk, 2 * nq), BF16),
            pltpu.VMEM((2 * nk, 2 * nq), BF16),
            pltpu.VMEM((NH, Z, 3, nr, 128), F32),
            pltpu.VMEM((NH, nr, 128), F32),
            pltpu.VMEM((NH, nr, 128), F32),
            pltpu.VMEM((NH, 2, Z, G, HD), F32),
            pltpu.VMEM((NH, 2, Z, G, HD), F32),
            pltpu.VMEM((NH, 2, Y, G, HD), F32),
            pltpu.VMEM((NH, 2, Y, G, HD), F32),
            pltpu.VMEM((NH, 4, 2, MR, 2, G, HD), BF16),
            pltpu.VMEM((NH, 4, 2, MR, 2, G, HD), BF16),
            pltpu.VMEM((NH, 3, 2, G, HD), F32),
            pltpu.VMEM((NH, 2, 3, 8, HD), F32),
            pltpu.VMEM((NH, 2, 3, 8, HD), F32),
            dma,
            dma((H - 1,)),
            dma((H - 1,)),
            dma((2,)),
            dma((2,)),
            dma((4 * NH + 2, 2, MR)),
            dma((4 * NH + 2, 2, MR)),
            dma((NH, Z - 1)),
            dma((NH, Z - 1)),
            dma((NH, 4, 2, MR)),
            dma((NH, 4, 2, MR)),
            dma((NH, 2)),
            dma((NH, 2)),
        ],
        compiler_params=pltpu.CompilerParams(
            collective_id=0, has_side_effects=True, vmem_limit_bytes=56 * 1024 * 1024
        ),
    )(raw, positions, filter_taps, grad_out)
    attn, grad = pl.pallas_call(
        hand_on,
        out_shape=(
            jax.ShapeDtypeStruct((rows, CW), BF16),
            jax.ShapeDtypeStruct((3, rows, CW), BF16),
        ),
        in_specs=[vmem, vmem],
        out_specs=(vmem, vmem),
    )(attn, grad)
    return attn, jnp.transpose(grad, (1, 0, 2))


def solution(mesh):
    n = mesh.shape["ctx"]
    Y = 1
    while (2 * Y) * (2 * Y) <= n and n % (2 * Y) == 0:
        Y *= 2
    in_specs = (P("ctx", None, "head"), P("ctx"), P(None, None, "head"), P(("ctx", "head"), None))
    out_specs = (P("ctx", "head"), P("ctx", None, "head"))
    return jax.shard_map(
        functools.partial(local, Y, n // Y, mesh.shape["head"]),
        mesh=mesh,
        in_specs=in_specs,
        out_specs=out_specs,
        check_vma=False,
    )
```

```python
import functools
import math

import jax
import jax.numpy as jnp
from jax import lax
from jax.experimental import pallas as pl
from jax.experimental.pallas import tpu as pltpu
from jax.sharding import PartitionSpec as P

HD = 128
MESH = pl.DeviceIdType.MESH
NEG = -1e30
F32 = jnp.float32
BF16 = jnp.bfloat16


def kernel(
    dims,
    raw_hbm,
    pos_hbm,
    taps_hbm,
    gout_ref,
    attn_ref,
    grad_ref,
    raw_ref,
    pos_ref,
    taps_ref,
    land,
    halo_raw,
    q_all,
    d_all,
    kv_all,
    k_code,
    w_all,
    s_all,
    p_low,
    x_low,
    stat_ml,
    stat_t,
    row_wt,
    row_fac,
    row_del,
    part_z,
    part_y,
    rs_out,
    rs_in,
    edge_out,
    edge_in,
    fin,
    halo_out,
    halo_in,
    load_sem,
    own_sem,
    a2a_send,
    a2a_recv,
    hr_send,
    hr_recv,
    ag_send,
    ag_recv,
    st_send,
    st_recv,
    rs_send,
    rs_recv,
    hg_send,
    hg_recv,
):
    Y, Z, H, G, NH, T = dims
    N = Y * Z
    d = lax.axis_index("ctx")
    hd = lax.axis_index("head")
    y = d // Z
    z = d % Z
    scaling = 1.0 / math.sqrt(HD)
    cexp = scaling * math.log2(math.e)

    d_next = (d + 1) % N
    d_prev = (d + N - 1) % N
    z_dev = lambda i: y * Z + i
    y_dev = lambda i: i * Z + z

    barrier = pltpu.get_barrier_semaphore()
    greet = [(z_dev((z + j) % Z), hd) for j in range(1, Z)]
    greet += [(y_dev((y + j) % Y), hd) for j in range(1, Y) if j <= 2 or Y - j <= 2]
    greet += [(d_next, hd), (d_prev, hd)]
    greet += [(d, (hd + j) % H) for j in range(1, H)]
    for dev in greet:
        pl.semaphore_signal(barrier, inc=1, device_id=dev, device_id_type=MESH)

    loads = [
        pltpu.make_async_copy(raw_hbm, raw_ref, load_sem.at[0]),
        pltpu.make_async_copy(taps_hbm, taps_ref, load_sem.at[1]),
        pltpu.make_async_copy(pos_hbm, pos_ref, load_sem.at[2]),
    ]
    for load in loads:
        load.start()

    def remote(src, dst, s_sem, r_sem, dev):
        return pltpu.make_async_remote_copy(
            src_ref=src, dst_ref=dst, send_sem=s_sem, recv_sem=r_sem, device_id=dev, device_id_type=MESH
        )

    tail_e = remote(
        raw_hbm.at[:, pl.ds(G - 16, 16)], halo_raw.at[0], hr_send.at[0], hr_recv.at[0], (d_next, hd)
    )
    tail_l = remote(
        raw_hbm.at[:, pl.ds(2 * G - 16, 16)], halo_raw.at[1], hr_send.at[1], hr_recv.at[1], (d_prev, hd)
    )
    RB = 2 * G // H
    CW = NH * HD

    def a2a(j):
        to = (hd + j) % H
        return remote(
            gout_ref.at[:, pl.ds(pl.multiple_of(to * CW, CW), CW)],
            land.at[pl.ds(pl.multiple_of(hd * RB, RB), RB)],
            a2a_send.at[j - 1],
            a2a_recv.at[j - 1],
            (d, to),
        )

    def a2a_in(j):
        frm = (hd + H - j) % H
        return remote(
            gout_ref.at[:, pl.ds(pl.multiple_of(hd * CW, CW), CW)],
            land.at[pl.ds(pl.multiple_of(frm * RB, RB), RB)],
            a2a_send.at[j - 1],
            a2a_recv.at[j - 1],
            (d, frm),
        )

    own = pltpu.make_async_copy(
        gout_ref.at[:, pl.ds(pl.multiple_of(hd * CW, CW), CW)],
        land.at[pl.ds(pl.multiple_of(hd * RB, RB), RB)],
        own_sem,
    )
    own.start()

    pl.semaphore_wait(barrier, len(greet))
    tail_e.start()
    tail_l.start()
    for j in range(1, H):
        a2a(j).start()
    for load in loads:
        load.wait()

    pair = pos_ref[0] // G
    rot = (pair - d + N) % N
    nk = Y * G
    nq = Z * G
    C = min(256, nq)
    group_of = lambda i: i >> (G.bit_length() - 1)

    def wrap(p):
        p = jnp.where(p >= 2 * N, p - 2 * N, p)
        return jnp.where(p >= N, p - N, p)

    def q_code(half, c):
        iq = lax.broadcasted_iota(jnp.int32, (1, C), 1) + c * C
        pq = wrap(group_of(iq) + (y * Z + rot))
        return pq * G + (iq & (G - 1)) if half == 0 else (iq & (G - 1)) - pq * G

    E = 16
    gathers = []
    for h in range(NH):
        gathers += [
            (lambda i, h=h: kv_all.at[0, h, :, i, pl.ds(E, G - E)], Y, y, y_dev),
            (lambda i, h=h: q_all.at[h, :, i, pl.ds(E, G - E)], Z, z, z_dev),
            (lambda i, h=h: kv_all.at[1, h, :, i, pl.ds(E, G - E)], Y, y, y_dev),
            (lambda i, h=h: d_all.at[h, :, i], Z, z, z_dev),
        ]
    gathers += [
        (lambda i: kv_all.at[:, :, :, i, pl.ds(0, E)], Y, y, y_dev),
        (lambda i: q_all.at[:, :, i, pl.ds(0, E)], Z, z, z_dev),
    ]
    K_EDGE, Q_EDGE = 4 * NH, 4 * NH + 1
    flips = [(h + f) % 2 for h in range(NH) for f in (0, 0, 1, 1)] + [0, 0]

    def steps_of(n, flip):
        a, b = n // 2, n - 1 - n // 2
        return (b, a) if flip else (a, b)

    def ag_copy(item, way, dist, incoming=False):
        view, n, me, dev_of = gathers[item]
        sign = 1 if way == 0 else n - 1
        hop = dist if dist <= 2 else dist - 2
        if incoming:
            slot = (me + (n - sign) * dist) % n
        else:
            slot = me if dist <= 2 else (me + (n - sign) * 2) % n
        dev = (dev_of((me + sign * hop) % n), hd)
        return remote(
            view(slot), view(slot), ag_send.at[item, way, dist - 1], ag_recv.at[item, way, dist - 1], dev
        )

    def ag_counts(item):
        return enumerate(steps_of(gathers[item][1], flips[item]))

    def ag_first(item):
        for dist in (2, 1):
            for way, count in ag_counts(item):
                if dist <= count:
                    ag_copy(item, way, dist).start()

    def ag_relay(item):
        for way, count in ag_counts(item):
            if count >= 2:
                ag_copy(item, way, 2, True).wait_recv()
            for dist in (4, 3):
                if dist <= count:
                    ag_copy(item, way, dist).start()

    def ag_last(item):
        for way, count in ag_counts(item):
            for dist in (1, 3, 4):
                if dist <= count:
                    ag_copy(item, way, dist, True).wait_recv()

    zero_rows = jnp.zeros((16, CW), F32)

    def featurize(kind, half, prior, rows):
        x = raw_ref[kind, pl.ds(half * G, rows)].astype(F32)
        row = lax.broadcasted_iota(jnp.int32, (rows, CW), 0)
        tap = taps_ref[kind]
        out = tap[0:1] * x
        for t in range(1, T):
            moved = pltpu.roll(x, t, 0)
            if prior is not None:
                for i in range(t):
                    moved = jnp.where(row == i, prior[16 - t + i : 17 - t + i], moved)
            out = out + tap[t : t + 1] * moved
        return out.astype(BF16)

    def own_view(kind, h, half):
        return q_all.at[h, half, z] if kind == 0 else kv_all.at[kind - 1, h, half, y]

    for kind in (1, 0, 2):
        for half in range(2):
            out = featurize(kind, half, None, G)
            for h in range(NH):
                own_view(kind, h, half)[pl.ds(E, G - E)] = out[E:, h * HD : (h + 1) * HD]

    for h in range(NH):
        ag_first(4 * h)
        ag_first(4 * h + 1)
    for h in range(NH):
        ag_first(4 * h + 2)

    tail_e.wait_recv()
    tail_l.wait_recv()
    for kind in range(3):
        for half in range(2):
            if half == 0:
                prior = jnp.where(pair == 0, zero_rows, halo_raw[0, kind].astype(F32))
            else:
                prior = jnp.where(
                    pair == N - 1, raw_ref[kind, pl.ds(G - 16, 16)].astype(F32), halo_raw[1, kind].astype(F32)
                )
            out = featurize(kind, half, prior, E)
            for h in range(NH):
                own_view(kind, h, half)[pl.ds(0, E)] = out[:, h * HD : (h + 1) * HD]
    ag_first(K_EDGE)
    ag_first(Q_EDGE)
    own.wait()
    for j in range(1, H):
        a2a_in(j).wait_recv()
    for half in range(2):
        for h in range(NH):
            d_all[h, half, z] = land[pl.ds(half * G, G), h * HD : (h + 1) * HD]
    for h in range(NH):
        ag_first(4 * h + 3)

    ik = lax.broadcasted_iota(jnp.int32, (nk, C), 0)
    pk = wrap(group_of(ik) * Z + (z + rot))
    k_code[0] = pk * G + (ik & (G - 1))
    k_code[1] = (ik & (G - 1)) - pk * G

    NT = (((1,), (1,)), ((), ()))
    TN = (((0,), (0,)), ((), ()))
    NN = (((1,), (0,)), ((), ()))

    def mm(a, b, how):
        return lax.dot_general(a, b, how, preferred_element_type=F32)

    zc = C // G
    lanes = C // 128

    def cols_of(half, c):
        return pl.ds(half * nq + c * C, C)

    def put_rows(ref, half, c, val):
        for i in range(lanes):
            ref[pl.ds((half * nq + c * C) // 128 + i, 1)] = val[:, i * 128 : (i + 1) * 128]

    def pass_score(h, half, c):
        q = q_all[h, half, pl.ds(c * zc, zc)].reshape(C, HD)
        score = []
        for kh in range(half + 1):
            sc = mm(kv_all[0, h, kh].reshape(nk, HD), q, NT)
            if kh == half:
                sc = jnp.where(k_code[half] <= q_code(half, c), sc, NEG)
            score.append(sc)
        top = jnp.max(score[0], axis=0, keepdims=True)
        if half == 1:
            top = jnp.maximum(top, jnp.max(score[1], axis=0, keepdims=True))
        total = jnp.zeros((1, C), F32)
        for kh in range(half + 1):
            w = jnp.exp2((score[kh] - top) * cexp)
            w_all[h, pl.ds(kh * nk, nk), cols_of(half, c)] = w
            total = total + jnp.sum(w, axis=0, keepdims=True)
        put_rows(stat_ml.at[h, z, 0], half, c, top)
        put_rows(stat_ml.at[h, z, 1], half, c, total)

    def pass_slope(h, half, c):
        g = d_all[h, half, pl.ds(c * zc, zc)].reshape(C, HD)
        tilt = jnp.zeros((1, C), F32)
        for kh in range(half + 1):
            slope = mm(kv_all[1, h, kh].reshape(nk, HD), g, NT)
            s_all[h, pl.ds(kh * nk, nk), cols_of(half, c)] = slope
            w = w_all[h, pl.ds(kh * nk, nk), cols_of(half, c)]
            tilt = tilt + jnp.sum(w * slope, axis=0, keepdims=True)
        put_rows(stat_t.at[h, z], half, c, tilt)

    def st_copy(which, h, j, incoming=False):
        slot = (z + Z - j) % Z if incoming else z
        dev = z_dev((z + Z - j) % Z if incoming else (z + j) % Z)
        ref = (stat_ml if which == 0 else stat_t).at[h, slot]
        return remote(ref, ref, st_send.at[which, h, j - 1], st_recv.at[which, h, j - 1], (dev, hd))

    def st_start(which, h):
        for j in sorted(range(1, Z), key=lambda j: -min(j, Z - j)):
            st_copy(which, h, j).start()

    def st_wait(which, h):
        for j in range(1, Z):
            st_copy(which, h, j, True).wait_recv()

    def st_finish_ml(h):
        st_wait(0, h)
        top = stat_ml[h, 0, 0]
        for i in range(1, Z):
            top = jnp.maximum(top, stat_ml[h, i, 0])
        total = jnp.zeros_like(top)
        rise = []
        for i in range(Z):
            rise.append(jnp.exp2((stat_ml[h, i, 0] - top) * cexp))
            total = total + stat_ml[h, i, 1] * rise[i]
        inv = 1.0 / total
        for i in range(Z):
            row_wt[h, i] = rise[i] * inv
        row_fac[h] = row_wt[h, z]

    def st_finish_t(h):
        st_wait(1, h)
        tilt = stat_t[h, 0] * row_wt[h, 0]
        for i in range(1, Z):
            tilt = tilt + stat_t[h, i] * row_wt[h, i]
        row_del[h] = tilt

    def row_of(ref, h, a, b):
        return jnp.concatenate([ref[h, pl.ds(i, 1)] for i in range(a // 128, b // 128)], axis=1)

    KC = min(256, nk)
    kz = KC // G

    def key_block(kh, c):
        lo = 0 if kh == 0 else nq
        return pl.ds(kh * nk + c * KC, KC), lo, pl.ds(lo, 2 * nq - lo)

    def of_queries(buf, h, kh):
        return buf[h].reshape(2 * nq, HD) if kh == 0 else buf[h, 1].reshape(nq, HD)

    def of_keys(kind, h, half):
        return kv_all[kind, h].reshape(2 * nk, HD) if half == 1 else kv_all[kind, h, 0].reshape(nk, HD)

    def pass_probs(h, kh, c):
        rows, lo, cols = key_block(kh, c)
        p = w_all[h, rows, cols] * row_of(row_fac, h, lo, 2 * nq)
        w_all[h, rows, cols] = p
        pb = p.astype(BF16)
        p_low[rows, cols] = pb
        part_y[1, h, kh, pl.ds(c * kz, kz)] = mm(pb, of_queries(d_all, h, kh), NN).reshape(kz, G, HD)

    def pass_out(h, half):
        p = p_low[pl.ds(0, nk * (half + 1)), pl.ds(half * nq, nq)]
        part_z[1, h, half] = mm(p, of_keys(1, h, half), TN).reshape(Z, G, HD)

    def pass_dscores(h, kh, c):
        rows, lo, cols = key_block(kh, c)
        x = w_all[h, rows, cols] * (s_all[h, rows, cols] - row_of(row_del, h, lo, 2 * nq))
        xb = x.astype(BF16)
        x_low[rows, cols] = xb
        part_y[0, h, kh, pl.ds(c * kz, kz)] = (mm(xb, of_queries(q_all, h, kh), NN) * scaling).reshape(kz, G, HD)

    def pass_dq(h, half):
        x = x_low[pl.ds(0, nk * (half + 1)), pl.ds(half * nq, nq)]
        part_z[0, h, half] = (mm(x, of_keys(0, h, half), TN) * scaling).reshape(Z, G, HD)

    def dq_like(which):
        return (part_z, Z, z, z_dev) if which == "z" else (part_y, Y, y, y_dev)

    O_ALL, Q_REST, K_REST, V_ALL, DK_EDGE, DQ_EDGE = range(6)

    def sum_of(h, item):
        r = E if h == NH - 1 else 0
        a, b = h % 2, (h + 1) % 2
        return (
            ("z", 1, 0, G, a),
            ("z", 0, r, G - r, a),
            ("y", 0, r, G - r, a),
            ("y", 1, 0, G, a),
            ("y", 0, 0, E, b),
            ("z", 0, 0, E, b),
        )[item]

    def items_of(h):
        return range(6 if h == NH - 1 else 4)

    def rs_bufs(h, item, way, dist):
        which, kind, row0, rows, flip = sum_of(h, item)
        if item >= DK_EDGE:
            return edge_out.at[item - DK_EDGE, way, dist - 1], edge_in.at[item - DK_EDGE, way, dist - 1]
        at = (h, item, way, dist - 1, slice(None), pl.ds(row0, rows))
        return rs_out.at[at], rs_in.at[at]

    def rs_copy(h, item, way, dist):
        part, n, me, dev_of = dq_like(sum_of(h, item)[0])
        sign = 1 if way == 0 else n - 1
        hop = dist if dist <= 2 else dist - 2
        src, dst = rs_bufs(h, item, way, dist)
        return remote(
            src,
            dst,
            rs_send.at[h, item, way, dist - 1],
            rs_recv.at[h, item, way, dist - 1],
            (dev_of((me + sign * hop) % n), hd),
        )

    def rs_counts(h, item):
        which, kind, row0, rows, flip = sum_of(h, item)
        return enumerate(steps_of(Z if which == "z" else Y, flip))

    def rs_part(h, item, dest):
        which, kind, row0, rows, flip = sum_of(h, item)
        return dq_like(which)[0][kind, h, :, pl.ds(dest, 1), pl.ds(row0, rows)].reshape(2, rows, HD)

    def rs_put(h, item, way, dist):
        part, n, me, dev_of = dq_like(sum_of(h, item)[0])
        sign = 1 if way == 0 else n - 1
        val = rs_part(h, item, (me + sign * dist) % n)
        if dist == 2:
            count = steps_of(n, sum_of(h, item)[4])[way]
            for more in (3, 4):
                if more <= count:
                    rs_copy(h, item, way, more).wait_recv()
                    val = val + rs_bufs(h, item, way, more)[1][...].astype(F32)
        rs_bufs(h, item, way, dist)[0][...] = val.astype(BF16)
        rs_copy(h, item, way, dist).start()

    def rs_first(h, item):
        for dist in (4, 3, 1):
            for way, count in rs_counts(h, item):
                if dist <= count:
                    rs_put(h, item, way, dist)

    def rs_relay(h, item):
        for way, count in rs_counts(h, item):
            if count >= 2:
                rs_put(h, item, way, 2)

    def rs_final(h, item):
        val = rs_part(h, item, z if sum_of(h, item)[0] == "z" else y)
        for way, count in rs_counts(h, item):
            for dist in (1, 2):
                if dist <= count:
                    rs_copy(h, item, way, dist).wait_recv()
                    val = val + rs_bufs(h, item, way, dist)[1][...].astype(F32)
        return val

    def hg_copy(h, half):
        return remote(
            halo_out.at[h, half],
            halo_in.at[h, half],
            hg_send.at[h, half],
            hg_recv.at[h, half],
            (d_prev if half == 0 else d_next, hd),
        )

    def send_halo(h):
        for kind in range(3):
            for half in range(2):
                halo_out[h, half, kind] = fin[h, kind, half, 0:8]
        for half in range(2):
            hg_copy(h, half).start()

    def finish_edges(h):
        for kind, item in ((1, DK_EDGE), (0, DQ_EDGE)):
            fin[h, kind, :, pl.ds(0, E)] = rs_final(h, item)

    def finish_sums(h, items):
        for item in items:
            val = rs_final(h, item)
            if item == O_ALL:
                for half in range(2):
                    attn_ref[pl.ds(half * G, G), h * HD : (h + 1) * HD] = val[half].astype(BF16)
            else:
                which, kind, row0, rows, flip = sum_of(h, item)
                fin[h, {Q_REST: 0, K_REST: 1, V_ALL: 2}[item], :, pl.ds(row0, rows)] = val

    row1 = lax.broadcasted_iota(jnp.int32, (G, HD), 0)

    def finish_grads(h):
        for half in range(2):
            hg_copy(h, half).wait_recv()
        for kind in range(3):
            tap = taps_ref[kind][:, h * HD : (h + 1) * HD]
            for half in range(2):
                x = fin[h, kind, half]
                if half == 0:
                    nxt = jnp.where(pair == N - 1, fin[h, kind, 1, 0:8], halo_in[h, 0, kind])
                else:
                    nxt = jnp.where(pair == 0, jnp.zeros((8, HD), F32), halo_in[h, 1, kind])
                out = tap[0:1] * x
                for t in range(1, T):
                    moved = pltpu.roll(x, G - t, 0)
                    for i in range(t):
                        moved = jnp.where(row1 == G - t + i, nxt[i : i + 1], moved)
                    out = out + tap[t : t + 1] * moved
                grad_ref[kind, pl.ds(half * G, G), h * HD : (h + 1) * HD] = out.astype(BF16)

    nc = nq // C
    kc = nk // KC
    chunks = [(1, c) for c in range(nc)] + [(0, c) for c in range(nc)]
    for item in (0, 1, 4, 5, 2, 6, K_EDGE, Q_EDGE, 3, 7):
        ag_relay(item)
    for item in (0, 1, K_EDGE, Q_EDGE):
        ag_last(item)
    for half, c in chunks:
        pass_score(0, half, c)
    st_start(0, 0)
    ag_last(4)
    ag_last(5)
    for half, c in chunks:
        pass_score(1, half, c)
    st_start(0, 1)
    for h in range(NH):
        ag_last(4 * h + 2)
        ag_last(4 * h + 3)
        for half, c in chunks:
            pass_slope(h, half, c)
        st_start(1, h)
    for h in range(NH):
        st_finish_ml(h)
        for kh in range(2):
            for c in range(kc):
                pass_probs(h, kh, c)
        rs_first(h, V_ALL)
        for half in range(2):
            pass_out(h, half)
        rs_first(h, O_ALL)
    for h in range(NH):
        st_finish_t(h)
        for kh in range(2):
            for c in range(kc):
                pass_dscores(h, kh, c)
        if h == NH - 1:
            rs_first(h, DK_EDGE)
        rs_first(h, K_REST)
        for half in range(2):
            pass_dq(h, half)
        if h == NH - 1:
            rs_first(h, DQ_EDGE)
        rs_first(h, Q_REST)
    for h in range(NH):
        rs_relay(h, V_ALL)
        rs_relay(h, O_ALL)
    for h, item in ((0, K_REST), (0, Q_REST), (1, DK_EDGE), (1, DQ_EDGE), (1, K_REST), (1, Q_REST)):
        rs_relay(h, item)
    finish_sums(0, (V_ALL, O_ALL))
    finish_sums(1, (V_ALL, O_ALL))
    finish_sums(0, (K_REST, Q_REST))
    send_halo(0)
    finish_edges(1)
    send_halo(1)
    finish_sums(1, (K_REST, Q_REST))
    finish_grads(0)
    finish_grads(1)

    tail_e.wait_send()
    tail_l.wait_send()
    for j in range(1, H):
        a2a(j).wait_send()
    for item in range(len(gathers)):
        for way, count in ag_counts(item):
            for dist in range(1, count + 1):
                ag_copy(item, way, dist).wait_send()
    for h in range(NH):
        for item in items_of(h):
            for way, count in rs_counts(h, item):
                for dist in range(1, count + 1):
                    rs_copy(h, item, way, dist).wait_send()
        for j in range(1, Z):
            st_copy(0, h, j).wait_send()
            st_copy(1, h, j).wait_send()
        for half in range(2):
            hg_copy(h, half).wait_send()


def hand_on(attn_in, grad_in, attn_out, grad_out):
    attn_out[...] = attn_in[...]
    grad_out[...] = grad_in[...]


def local(Y, Z, H, qkv_raw, positions, filter_taps, grad_out):
    rows = positions.shape[0]
    G = rows // 2
    CW = qkv_raw.shape[2]
    NH = CW // HD
    T = filter_taps.shape[1]
    MR = max(Y, Z) // 2
    nq, nk = Z * G, Y * G
    C = min(256, nq)
    nr = 2 * nq // 128
    raw = jnp.transpose(qkv_raw, (1, 0, 2))
    dma = pltpu.SemaphoreType.DMA
    vmem = pl.BlockSpec(memory_space=pltpu.VMEM)
    attn, grad = pl.pallas_call(
        functools.partial(kernel, (Y, Z, H, G, NH, T)),
        out_shape=(
            jax.ShapeDtypeStruct((rows, CW), BF16),
            jax.ShapeDtypeStruct((3, rows, CW), BF16),
        ),
        in_specs=[pl.BlockSpec(memory_space=pltpu.HBM)] * 4,
        out_specs=(vmem, vmem),
        scratch_shapes=[
            pltpu.VMEM((3, rows, CW), BF16),
            pltpu.SMEM((rows,), jnp.int32),
            pltpu.VMEM(filter_taps.shape, F32),
            pltpu.VMEM((rows, CW), BF16),
            pltpu.VMEM((2, 3, 16, CW), BF16),
            pltpu.VMEM((NH, 2, Z, G, HD), BF16),
            pltpu.VMEM((NH, 2, Z, G, HD), BF16),
            pltpu.VMEM((2, NH, 2, Y, G, HD), BF16),
            pltpu.VMEM((2, nk, C), jnp.int32),
            pltpu.VMEM((NH, 2 * nk, 2 * nq), F32),
            pltpu.VMEM((NH, 2 * nk, 2 * nq), F32),
            pltpu.VMEM((2 * nk, 2 * nq), BF16),
            pltpu.VMEM((2 * nk, 2 * nq), BF16),
            pltpu.VMEM((NH, Z, 2, nr, 128), F32),
            pltpu.VMEM((NH, Z, nr, 128), F32),
            pltpu.VMEM((NH, Z, nr, 128), F32),
            pltpu.VMEM((NH, nr, 128), F32),
            pltpu.VMEM((NH, nr, 128), F32),
            pltpu.VMEM((2, NH, 2, Z, G, HD), F32),
            pltpu.VMEM((2, NH, 2, Y, G, HD), F32),
            pltpu.VMEM((NH, 4, 2, MR, 2, G, HD), BF16),
            pltpu.VMEM((NH, 4, 2, MR, 2, G, HD), BF16),
            pltpu.VMEM((2, 2, MR, 2, 16, HD), BF16),
            pltpu.VMEM((2, 2, MR, 2, 16, HD), BF16),
            pltpu.VMEM((NH, 3, 2, G, HD), F32),
            pltpu.VMEM((NH, 2, 3, 8, HD), F32),
            pltpu.VMEM((NH, 2, 3, 8, HD), F32),
            dma((3,)),
            dma,
            dma((H - 1,)),
            dma((H - 1,)),
            dma((2,)),
            dma((2,)),
            dma((4 * NH + 2, 2, MR)),
            dma((4 * NH + 2, 2, MR)),
            dma((2, NH, Z - 1)),
            dma((2, NH, Z - 1)),
            dma((NH, 6, 2, MR)),
            dma((NH, 6, 2, MR)),
            dma((NH, 2)),
            dma((NH, 2)),
        ],
        compiler_params=pltpu.CompilerParams(
            collective_id=0, has_side_effects=True, vmem_limit_bytes=56 * 1024 * 1024
        ),
    )(raw, positions, filter_taps, grad_out)
    attn, grad = pl.pallas_call(
        hand_on,
        out_shape=(
            jax.ShapeDtypeStruct((rows, CW), BF16),
            jax.ShapeDtypeStruct((3, rows, CW), BF16),
        ),
        in_specs=[vmem, vmem],
        out_specs=(vmem, vmem),
    )(attn, grad)
    return attn, jnp.transpose(grad, (1, 0, 2))


def solution(mesh):
    n = mesh.shape["ctx"]
    Y = 1
    while (2 * Y) * (2 * Y) <= n and n % (2 * Y) == 0:
        Y *= 2
    in_specs = (P("ctx", None, "head"), P("ctx"), P(None, None, "head"), P(("ctx", "head"), None))
    out_specs = (P("ctx", "head"), P("ctx", None, "head"))
    return jax.shard_map(
        functools.partial(local, Y, n // Y, mesh.shape["head"]),
        mesh=mesh,
        in_specs=in_specs,
        out_specs=out_specs,
        check_vma=False,
    )
```

```python
import functools
import math

import jax
import jax.numpy as jnp
from jax import lax
from jax.experimental import pallas as pl
from jax.experimental.pallas import tpu as pltpu
from jax.sharding import PartitionSpec as P

HD = 128
MESH = pl.DeviceIdType.MESH
NEG = -1e30
F32 = jnp.float32
BF16 = jnp.bfloat16


def kernel(
    dims,
    raw_hbm,
    pos_hbm,
    taps_hbm,
    gout_ref,
    attn_ref,
    grad_ref,
    raw_ref,
    pos_ref,
    taps_ref,
    land,
    halo_raw,
    q_all,
    d_all,
    kv_all,
    k_code,
    w_all,
    s_all,
    p_low,
    x_low,
    stat_ml,
    stat_t,
    row_wt,
    row_fac,
    row_del,
    part_z,
    part_y,
    rs_out,
    rs_in,
    edge_out,
    edge_in,
    fin,
    halo_out,
    halo_in,
    load_sem,
    own_sem,
    a2a_send,
    a2a_recv,
    hr_send,
    hr_recv,
    ag_send,
    ag_recv,
    st_send,
    st_recv,
    rs_send,
    rs_recv,
    hg_send,
    hg_recv,
):
    Y, Z, H, G, NH, T = dims
    N = Y * Z
    d = lax.axis_index("ctx")
    hd = lax.axis_index("head")
    y = d // Z
    z = d % Z
    scaling = 1.0 / math.sqrt(HD)
    cexp = scaling * math.log2(math.e)

    d_next = (d + 1) % N
    d_prev = (d + N - 1) % N
    z_dev = lambda i: y * Z + i
    y_dev = lambda i: i * Z + z

    barrier = pltpu.get_barrier_semaphore()
    greet = [(z_dev((z + j) % Z), hd) for j in range(1, Z)]
    greet += [(y_dev((y + j) % Y), hd) for j in range(1, Y)]
    greet += [(d_next, hd), (d_prev, hd)]
    greet += [(d, (hd + j) % H) for j in range(1, H)]
    for dev in greet:
        pl.semaphore_signal(barrier, inc=1, device_id=dev, device_id_type=MESH)

    loads = [
        pltpu.make_async_copy(raw_hbm, raw_ref, load_sem.at[0]),
        pltpu.make_async_copy(taps_hbm, taps_ref, load_sem.at[1]),
        pltpu.make_async_copy(pos_hbm, pos_ref, load_sem.at[2]),
    ]
    for load in loads:
        load.start()

    def remote(src, dst, s_sem, r_sem, dev):
        return pltpu.make_async_remote_copy(
            src_ref=src, dst_ref=dst, send_sem=s_sem, recv_sem=r_sem, device_id=dev, device_id_type=MESH
        )

    tail_e = remote(
        raw_hbm.at[:, pl.ds(G - 16, 16)], halo_raw.at[0], hr_send.at[0], hr_recv.at[0], (d_next, hd)
    )
    tail_l = remote(
        raw_hbm.at[:, pl.ds(2 * G - 16, 16)], halo_raw.at[1], hr_send.at[1], hr_recv.at[1], (d_prev, hd)
    )
    RB = 2 * G // H
    CW = NH * HD

    def a2a(j):
        to = (hd + j) % H
        return remote(
            gout_ref.at[:, pl.ds(pl.multiple_of(to * CW, CW), CW)],
            land.at[pl.ds(pl.multiple_of(hd * RB, RB), RB)],
            a2a_send.at[j - 1],
            a2a_recv.at[j - 1],
            (d, to),
        )

    def a2a_in(j):
        frm = (hd + H - j) % H
        return remote(
            gout_ref.at[:, pl.ds(pl.multiple_of(hd * CW, CW), CW)],
            land.at[pl.ds(pl.multiple_of(frm * RB, RB), RB)],
            a2a_send.at[j - 1],
            a2a_recv.at[j - 1],
            (d, frm),
        )

    own = pltpu.make_async_copy(
        gout_ref.at[:, pl.ds(pl.multiple_of(hd * CW, CW), CW)],
        land.at[pl.ds(pl.multiple_of(hd * RB, RB), RB)],
        own_sem,
    )
    own.start()

    pl.semaphore_wait(barrier, len(greet))
    tail_e.start()
    tail_l.start()
    for j in range(1, H):
        a2a(j).start()
    for load in loads:
        load.wait()

    pair = pos_ref[0] // G
    rot = (pair - d + N) % N
    nk = Y * G
    nq = Z * G
    C = min(256, nq)
    group_of = lambda i: i >> (G.bit_length() - 1)

    def wrap(p):
        p = jnp.where(p >= 2 * N, p - 2 * N, p)
        return jnp.where(p >= N, p - N, p)

    def q_code(half, c):
        iq = lax.broadcasted_iota(jnp.int32, (1, C), 1) + c * C
        pq = wrap(group_of(iq) + (y * Z + rot))
        return pq * G + (iq & (G - 1)) if half == 0 else (iq & (G - 1)) - pq * G

    E = 16
    gathers = []
    for h in range(NH):
        gathers += [
            (lambda i, h=h: kv_all.at[0, h, :, i, pl.ds(E, G - E)], Y, y, y_dev),
            (lambda i, h=h: q_all.at[h, :, i, pl.ds(E, G - E)], Z, z, z_dev),
            (lambda i, h=h: kv_all.at[1, h, :, i, pl.ds(E, G - E)], Y, y, y_dev),
            (lambda i, h=h: d_all.at[h, :, i], Z, z, z_dev),
        ]
    gathers += [
        (lambda i: kv_all.at[:, :, :, i, pl.ds(0, E)], Y, y, y_dev),
        (lambda i: q_all.at[:, :, i, pl.ds(0, E)], Z, z, z_dev),
    ]
    K_EDGE, Q_EDGE = 4 * NH, 4 * NH + 1
    flips = [(h + f) % 2 for h in range(NH) for f in (0, 0, 1, 1)] + [0, 0]

    def steps_of(n, flip):
        a, b = n // 2, n - 1 - n // 2
        return (b, a) if flip else (a, b)

    def ag_copy(item, way, dist, incoming=False):
        view, n, me, dev_of = gathers[item]
        sign = 1 if way == 0 else n - 1
        near = dist <= 2 or item >= K_EDGE
        hop = dist if near else dist - 2
        if incoming:
            slot = (me + (n - sign) * dist) % n
        else:
            slot = me if near else (me + (n - sign) * 2) % n
        dev = (dev_of((me + sign * hop) % n), hd)
        return remote(
            view(slot), view(slot), ag_send.at[item, way, dist - 1], ag_recv.at[item, way, dist - 1], dev
        )

    def ag_counts(item):
        return enumerate(steps_of(gathers[item][1], flips[item]))

    def ag_first(item):
        for dist in (4, 3, 2, 1) if item >= K_EDGE else (2, 1):
            for way, count in ag_counts(item):
                if dist <= count:
                    ag_copy(item, way, dist).start()

    def ag_relay(item):
        for way, count in ag_counts(item):
            if count >= 2:
                ag_copy(item, way, 2, True).wait_recv()
            for dist in (4, 3):
                if dist <= count:
                    ag_copy(item, way, dist).start()

    def ag_last(item):
        for way, count in ag_counts(item):
            for dist in (1, 2, 3, 4) if item >= K_EDGE else (1, 3, 4):
                if dist <= count:
                    ag_copy(item, way, dist, True).wait_recv()

    zero_rows = jnp.zeros((16, CW), F32)

    def featurize(kind, half, prior, rows):
        x = raw_ref[kind, pl.ds(half * G, rows)].astype(F32)
        row = lax.broadcasted_iota(jnp.int32, (rows, CW), 0)
        tap = taps_ref[kind]
        out = tap[0:1] * x
        for t in range(1, T):
            moved = pltpu.roll(x, t, 0)
            if prior is not None:
                for i in range(t):
                    moved = jnp.where(row == i, prior[16 - t + i : 17 - t + i], moved)
            out = out + tap[t : t + 1] * moved
        return out.astype(BF16)

    def own_view(kind, h, half):
        return q_all.at[h, half, z] if kind == 0 else kv_all.at[kind - 1, h, half, y]

    for item, kind in enumerate((1, 0, 2)):
        for half in range(2):
            out = featurize(kind, half, None, G)
            for h in range(NH):
                own_view(kind, h, half)[pl.ds(E, G - E)] = out[E:, h * HD : (h + 1) * HD]
        for h in range(NH):
            ag_first(4 * h + item)

    tail_e.wait_recv()
    tail_l.wait_recv()
    for kind in range(3):
        for half in range(2):
            if half == 0:
                prior = jnp.where(pair == 0, zero_rows, halo_raw[0, kind].astype(F32))
            else:
                prior = jnp.where(
                    pair == N - 1, raw_ref[kind, pl.ds(G - 16, 16)].astype(F32), halo_raw[1, kind].astype(F32)
                )
            out = featurize(kind, half, prior, E)
            for h in range(NH):
                own_view(kind, h, half)[pl.ds(0, E)] = out[:, h * HD : (h + 1) * HD]
    ag_first(K_EDGE)
    ag_first(Q_EDGE)
    own.wait()
    for j in range(1, H):
        a2a_in(j).wait_recv()
    for half in range(2):
        for h in range(NH):
            d_all[h, half, z] = land[pl.ds(half * G, G), h * HD : (h + 1) * HD]
    for h in range(NH):
        ag_first(4 * h + 3)

    ik = lax.broadcasted_iota(jnp.int32, (nk, C), 0)
    pk = wrap(group_of(ik) * Z + (z + rot))
    k_code[0] = pk * G + (ik & (G - 1))
    k_code[1] = (ik & (G - 1)) - pk * G

    NT = (((1,), (1,)), ((), ()))
    TN = (((0,), (0,)), ((), ()))
    NN = (((1,), (0,)), ((), ()))

    def mm(a, b, how):
        return lax.dot_general(a, b, how, preferred_element_type=F32)

    zc = C // G
    lanes = C // 128

    def cols_of(half, c):
        return pl.ds(half * nq + c * C, C)

    def put_rows(ref, half, c, val):
        for i in range(lanes):
            ref[pl.ds((half * nq + c * C) // 128 + i, 1)] = val[:, i * 128 : (i + 1) * 128]

    def pass_score(h, half, c):
        q = q_all[h, half, pl.ds(c * zc, zc)].reshape(C, HD)
        score = []
        for kh in range(half + 1):
            sc = mm(kv_all[0, h, kh].reshape(nk, HD), q, NT)
            if kh == half:
                sc = jnp.where(k_code[half] <= q_code(half, c), sc, NEG)
            score.append(sc)
        top = jnp.max(score[0], axis=0, keepdims=True)
        if half == 1:
            top = jnp.maximum(top, jnp.max(score[1], axis=0, keepdims=True))
        total = jnp.zeros((1, C), F32)
        for kh in range(half + 1):
            w = jnp.exp2((score[kh] - top) * cexp)
            w_all[h, pl.ds(kh * nk, nk), cols_of(half, c)] = w
            total = total + jnp.sum(w, axis=0, keepdims=True)
        put_rows(stat_ml.at[h, z, 0], half, c, top)
        put_rows(stat_ml.at[h, z, 1], half, c, total)

    def pass_slope(h, half, c):
        g = d_all[h, half, pl.ds(c * zc, zc)].reshape(C, HD)
        tilt = jnp.zeros((1, C), F32)
        for kh in range(half + 1):
            slope = mm(kv_all[1, h, kh].reshape(nk, HD), g, NT)
            s_all[h, pl.ds(kh * nk, nk), cols_of(half, c)] = slope
            w = w_all[h, pl.ds(kh * nk, nk), cols_of(half, c)]
            tilt = tilt + jnp.sum(w * slope, axis=0, keepdims=True)
        put_rows(stat_t.at[h, z], half, c, tilt)

    def st_copy(which, h, j, incoming=False):
        slot = (z + Z - j) % Z if incoming else z
        dev = z_dev((z + Z - j) % Z if incoming else (z + j) % Z)
        ref = (stat_ml if which == 0 else stat_t).at[h, slot]
        return remote(ref, ref, st_send.at[which, h, j - 1], st_recv.at[which, h, j - 1], (dev, hd))

    def st_start(which, h):
        for j in sorted(range(1, Z), key=lambda j: -min(j, Z - j)):
            st_copy(which, h, j).start()

    def st_wait(which, h):
        for j in range(1, Z):
            st_copy(which, h, j, True).wait_recv()

    def st_finish_ml(h):
        st_wait(0, h)
        top = stat_ml[h, 0, 0]
        for i in range(1, Z):
            top = jnp.maximum(top, stat_ml[h, i, 0])
        total = jnp.zeros_like(top)
        rise = []
        for i in range(Z):
            rise.append(jnp.exp2((stat_ml[h, i, 0] - top) * cexp))
            total = total + stat_ml[h, i, 1] * rise[i]
        inv = 1.0 / total
        for i in range(Z):
            row_wt[h, i] = rise[i] * inv
        row_fac[h] = row_wt[h, z]

    def st_finish_t(h):
        st_wait(1, h)
        tilt = stat_t[h, 0] * row_wt[h, 0]
        for i in range(1, Z):
            tilt = tilt + stat_t[h, i] * row_wt[h, i]
        row_del[h] = tilt

    def row_of(ref, h, a, b):
        return jnp.concatenate([ref[h, pl.ds(i, 1)] for i in range(a // 128, b // 128)], axis=1)

    KC = min(256, nk)
    kz = KC // G

    def key_block(kh, c):
        lo = 0 if kh == 0 else nq
        return pl.ds(kh * nk + c * KC, KC), lo, pl.ds(lo, 2 * nq - lo)

    def of_queries(buf, h, kh):
        return buf[h].reshape(2 * nq, HD) if kh == 0 else buf[h, 1].reshape(nq, HD)

    def of_keys(kind, h, half):
        return kv_all[kind, h].reshape(2 * nk, HD) if half == 1 else kv_all[kind, h, 0].reshape(nk, HD)

    def pass_probs(h, kh, c):
        rows, lo, cols = key_block(kh, c)
        p = w_all[h, rows, cols] * row_of(row_fac, h, lo, 2 * nq)
        w_all[h, rows, cols] = p
        pb = p.astype(BF16)
        p_low[rows, cols] = pb
        part_y[1, h, kh, pl.ds(c * kz, kz)] = mm(pb, of_queries(d_all, h, kh), NN).reshape(kz, G, HD)

    def pass_out(h, half):
        p = p_low[pl.ds(0, nk * (half + 1)), pl.ds(half * nq, nq)]
        part_z[1, h, half] = mm(p, of_keys(1, h, half), TN).reshape(Z, G, HD)

    def pass_dscores(h, kh, c):
        rows, lo, cols = key_block(kh, c)
        x = w_all[h, rows, cols] * (s_all[h, rows, cols] - row_of(row_del, h, lo, 2 * nq))
        xb = x.astype(BF16)
        x_low[rows, cols] = xb
        part_y[0, h, kh, pl.ds(c * kz, kz)] = (mm(xb, of_queries(q_all, h, kh), NN) * scaling).reshape(kz, G, HD)

    def pass_dq(h, half):
        x = x_low[pl.ds(0, nk * (half + 1)), pl.ds(half * nq, nq)]
        part_z[0, h, half] = (mm(x, of_keys(0, h, half), TN) * scaling).reshape(Z, G, HD)

    def dq_like(which):
        return (part_z, Z, z, z_dev) if which == "z" else (part_y, Y, y, y_dev)

    O_ALL, Q_REST, K_REST, V_REST, DQ_EDGE, DK_EDGE, DV_EDGE = range(7)

    def sum_of(h, item):
        a, b = h % 2, (h + 1) % 2
        return (
            ("z", 1, 0, G, a),
            ("z", 0, E, G - E, a),
            ("y", 0, E, G - E, a),
            ("y", 1, E, G - E, a),
            ("z", 0, 0, E, b),
            ("y", 0, 0, E, b),
            ("y", 1, 0, E, b),
        )[item]

    def rs_bufs(h, item, way, dist):
        which, kind, row0, rows, flip = sum_of(h, item)
        if item >= DQ_EDGE:
            at = (h, item - DQ_EDGE, way, dist - 1)
            return edge_out.at[at], edge_in.at[at]
        at = (h, item, way, dist - 1, slice(None), pl.ds(row0, rows))
        return rs_out.at[at], rs_in.at[at]

    def rs_copy(h, item, way, dist):
        part, n, me, dev_of = dq_like(sum_of(h, item)[0])
        sign = 1 if way == 0 else n - 1
        hop = dist if dist <= 2 or item >= DQ_EDGE else dist - 2
        src, dst = rs_bufs(h, item, way, dist)
        return remote(
            src,
            dst,
            rs_send.at[h, item, way, dist - 1],
            rs_recv.at[h, item, way, dist - 1],
            (dev_of((me + sign * hop) % n), hd),
        )

    def rs_counts(h, item):
        which, kind, row0, rows, flip = sum_of(h, item)
        return enumerate(steps_of(Z if which == "z" else Y, flip))

    def rs_part(h, item, dest):
        which, kind, row0, rows, flip = sum_of(h, item)
        return dq_like(which)[0][kind, h, :, pl.ds(dest, 1), pl.ds(row0, rows)].reshape(2, rows, HD)

    def rs_put(h, item, way, dist):
        part, n, me, dev_of = dq_like(sum_of(h, item)[0])
        sign = 1 if way == 0 else n - 1
        val = rs_part(h, item, (me + sign * dist) % n)
        if dist == 2 and item < DQ_EDGE:
            count = steps_of(n, sum_of(h, item)[4])[way]
            for more in (3, 4):
                if more <= count:
                    rs_copy(h, item, way, more).wait_recv()
                    val = val + rs_bufs(h, item, way, more)[1][...].astype(F32)
        rs_bufs(h, item, way, dist)[0][...] = val.astype(BF16)
        rs_copy(h, item, way, dist).start()

    def rs_first(h, item):
        for dist in (4, 3, 2, 1) if item >= DQ_EDGE else (4, 3, 1):
            for way, count in rs_counts(h, item):
                if dist <= count:
                    rs_put(h, item, way, dist)

    def rs_relay(h, item):
        for way, count in rs_counts(h, item):
            if count >= 2:
                rs_put(h, item, way, 2)

    def rs_final(h, item):
        val = rs_part(h, item, z if sum_of(h, item)[0] == "z" else y)
        for way, count in rs_counts(h, item):
            for dist in (1, 2, 3, 4) if item >= DQ_EDGE else (1, 2):
                if dist <= count:
                    rs_copy(h, item, way, dist).wait_recv()
                    val = val + rs_bufs(h, item, way, dist)[1][...].astype(F32)
        return val

    def hg_copy(h, half):
        return remote(
            halo_out.at[h, half],
            halo_in.at[h, half],
            hg_send.at[h, half],
            hg_recv.at[h, half],
            (d_prev if half == 0 else d_next, hd),
        )

    def send_halo(h):
        for kind in range(3):
            for half in range(2):
                halo_out[h, half, kind] = fin[h, kind, half, 0:8]
        for half in range(2):
            hg_copy(h, half).start()

    def finish_edges(h):
        for kind, item in ((2, DV_EDGE), (1, DK_EDGE), (0, DQ_EDGE)):
            fin[h, kind, :, pl.ds(0, E)] = rs_final(h, item)

    def finish_sums(h, items):
        for item in items:
            val = rs_final(h, item)
            if item == O_ALL:
                for half in range(2):
                    attn_ref[pl.ds(half * G, G), h * HD : (h + 1) * HD] = val[half].astype(BF16)
            else:
                which, kind, row0, rows, flip = sum_of(h, item)
                fin[h, {Q_REST: 0, K_REST: 1, V_REST: 2}[item], :, pl.ds(row0, rows)] = val

    row1 = lax.broadcasted_iota(jnp.int32, (G, HD), 0)

    def finish_grads(h):
        for half in range(2):
            hg_copy(h, half).wait_recv()
        for kind in range(3):
            tap = taps_ref[kind][:, h * HD : (h + 1) * HD]
            for half in range(2):
                x = fin[h, kind, half]
                if half == 0:
                    nxt = jnp.where(pair == N - 1, fin[h, kind, 1, 0:8], halo_in[h, 0, kind])
                else:
                    nxt = jnp.where(pair == 0, jnp.zeros((8, HD), F32), halo_in[h, 1, kind])
                out = tap[0:1] * x
                for t in range(1, T):
                    moved = pltpu.roll(x, G - t, 0)
                    for i in range(t):
                        moved = jnp.where(row1 == G - t + i, nxt[i : i + 1], moved)
                    out = out + tap[t : t + 1] * moved
                grad_ref[kind, pl.ds(half * G, G), h * HD : (h + 1) * HD] = out.astype(BF16)

    nc = nq // C
    kc = nk // KC
    chunks = [(1, c) for c in range(nc)] + [(0, c) for c in range(nc)]
    for item in (0, 1, 4, 5, 2, 6, 3, 7):
        ag_relay(item)
    for item in (0, 1, K_EDGE, Q_EDGE):
        ag_last(item)
    for half, c in chunks:
        pass_score(0, half, c)
    st_start(0, 0)
    ag_last(4)
    ag_last(5)
    for half, c in chunks:
        pass_score(1, half, c)
    st_start(0, 1)
    for h in range(NH):
        ag_last(4 * h + 2)
        ag_last(4 * h + 3)
        for half, c in chunks:
            pass_slope(h, half, c)
        st_start(1, h)
    for h in range(NH):
        st_finish_ml(h)
        for kh in range(2):
            for c in range(kc):
                pass_probs(h, kh, c)
        rs_first(h, DV_EDGE)
        rs_first(h, V_REST)
        for half in range(2):
            pass_out(h, half)
        rs_first(h, O_ALL)
    for h in range(NH):
        st_finish_t(h)
        for kh in range(2):
            for c in range(kc):
                pass_dscores(h, kh, c)
        rs_first(h, DK_EDGE)
        rs_first(h, K_REST)
        for half in range(2):
            pass_dq(h, half)
        rs_first(h, DQ_EDGE)
        rs_first(h, Q_REST)
    for h in range(NH):
        rs_relay(h, V_REST)
        rs_relay(h, O_ALL)
    for h in range(NH):
        rs_relay(h, K_REST)
        rs_relay(h, Q_REST)
    for h in range(NH):
        finish_edges(h)
        send_halo(h)
    for h in range(NH):
        finish_sums(h, (V_REST, O_ALL))
    for h in range(NH):
        finish_sums(h, (K_REST, Q_REST))
    finish_grads(0)
    finish_grads(1)

    tail_e.wait_send()
    tail_l.wait_send()
    for j in range(1, H):
        a2a(j).wait_send()
    for item in range(len(gathers)):
        for way, count in ag_counts(item):
            for dist in range(1, count + 1):
                ag_copy(item, way, dist).wait_send()
    for h in range(NH):
        for item in range(7):
            for way, count in rs_counts(h, item):
                for dist in range(1, count + 1):
                    rs_copy(h, item, way, dist).wait_send()
        for j in range(1, Z):
            st_copy(0, h, j).wait_send()
            st_copy(1, h, j).wait_send()
        for half in range(2):
            hg_copy(h, half).wait_send()


def hand_on(attn_in, grad_in, attn_out, grad_out):
    attn_out[...] = attn_in[...]
    grad_out[...] = grad_in[...]


def local(Y, Z, H, qkv_raw, positions, filter_taps, grad_out):
    rows = positions.shape[0]
    G = rows // 2
    CW = qkv_raw.shape[2]
    NH = CW // HD
    T = filter_taps.shape[1]
    MR = max(Y, Z) // 2
    nq, nk = Z * G, Y * G
    C = min(256, nq)
    nr = 2 * nq // 128
    raw = jnp.transpose(qkv_raw, (1, 0, 2))
    dma = pltpu.SemaphoreType.DMA
    vmem = pl.BlockSpec(memory_space=pltpu.VMEM)
    attn, grad = pl.pallas_call(
        functools.partial(kernel, (Y, Z, H, G, NH, T)),
        out_shape=(
            jax.ShapeDtypeStruct((rows, CW), BF16),
            jax.ShapeDtypeStruct((3, rows, CW), BF16),
        ),
        in_specs=[pl.BlockSpec(memory_space=pltpu.HBM)] * 4,
        out_specs=(vmem, vmem),
        scratch_shapes=[
            pltpu.VMEM((3, rows, CW), BF16),
            pltpu.SMEM((rows,), jnp.int32),
            pltpu.VMEM(filter_taps.shape, F32),
            pltpu.VMEM((rows, CW), BF16),
            pltpu.VMEM((2, 3, 16, CW), BF16),
            pltpu.VMEM((NH, 2, Z, G, HD), BF16),
            pltpu.VMEM((NH, 2, Z, G, HD), BF16),
            pltpu.VMEM((2, NH, 2, Y, G, HD), BF16),
            pltpu.VMEM((2, nk, C), jnp.int32),
            pltpu.VMEM((NH, 2 * nk, 2 * nq), F32),
            pltpu.VMEM((NH, 2 * nk, 2 * nq), F32),
            pltpu.VMEM((2 * nk, 2 * nq), BF16),
            pltpu.VMEM((2 * nk, 2 * nq), BF16),
            pltpu.VMEM((NH, Z, 2, nr, 128), F32),
            pltpu.VMEM((NH, Z, nr, 128), F32),
            pltpu.VMEM((NH, Z, nr, 128), F32),
            pltpu.VMEM((NH, nr, 128), F32),
            pltpu.VMEM((NH, nr, 128), F32),
            pltpu.VMEM((2, NH, 2, Z, G, HD), F32),
            pltpu.VMEM((2, NH, 2, Y, G, HD), F32),
            pltpu.VMEM((NH, 4, 2, MR, 2, G, HD), BF16),
            pltpu.VMEM((NH, 4, 2, MR, 2, G, HD), BF16),
            pltpu.VMEM((NH, 3, 2, MR, 2, 16, HD), BF16),
            pltpu.VMEM((NH, 3, 2, MR, 2, 16, HD), BF16),
            pltpu.VMEM((NH, 3, 2, G, HD), F32),
            pltpu.VMEM((NH, 2, 3, 8, HD), F32),
            pltpu.VMEM((NH, 2, 3, 8, HD), F32),
            dma((3,)),
            dma,
            dma((H - 1,)),
            dma((H - 1,)),
            dma((2,)),
            dma((2,)),
            dma((4 * NH + 2, 2, MR)),
            dma((4 * NH + 2, 2, MR)),
            dma((2, NH, Z - 1)),
            dma((2, NH, Z - 1)),
            dma((NH, 7, 2, MR)),
            dma((NH, 7, 2, MR)),
            dma((NH, 2)),
            dma((NH, 2)),
        ],
        compiler_params=pltpu.CompilerParams(
            collective_id=0, has_side_effects=True, vmem_limit_bytes=56 * 1024 * 1024
        ),
    )(raw, positions, filter_taps, grad_out)
    attn, grad = pl.pallas_call(
        hand_on,
        out_shape=(
            jax.ShapeDtypeStruct((rows, CW), BF16),
            jax.ShapeDtypeStruct((3, rows, CW), BF16),
        ),
        in_specs=[vmem, vmem],
        out_specs=(vmem, vmem),
    )(attn, grad)
    return attn, jnp.transpose(grad, (1, 0, 2))


def solution(mesh):
    n = mesh.shape["ctx"]
    Y = 1
    while (2 * Y) * (2 * Y) <= n and n % (2 * Y) == 0:
        Y *= 2
    in_specs = (P("ctx", None, "head"), P("ctx"), P(None, None, "head"), P(("ctx", "head"), None))
    out_specs = (P("ctx", "head"), P("ctx", None, "head"))
    return jax.shard_map(
        functools.partial(local, Y, n // Y, mesh.shape["head"]),
        mesh=mesh,
        in_specs=in_specs,
        out_specs=out_specs,
        check_vma=False,
    )
```

```python
import functools
import math

import jax
import jax.numpy as jnp
from jax import lax
from jax.experimental import pallas as pl
from jax.experimental.pallas import tpu as pltpu
from jax.sharding import PartitionSpec as P

HD = 128
MESH = pl.DeviceIdType.MESH
NEG = -1e30
F32 = jnp.float32
BF16 = jnp.bfloat16


def kernel(
    dims,
    raw_hbm,
    pos_hbm,
    taps_hbm,
    gout_ref,
    attn_ref,
    grad_ref,
    raw_ref,
    pos_ref,
    taps_ref,
    land,
    halo_raw,
    q_all,
    d_all,
    kv_all,
    k_code,
    w_all,
    s_all,
    p_low,
    x_low,
    stat_ml,
    stat_t,
    row_wt,
    row_fac,
    row_del,
    part_z,
    part_y,
    rs_out,
    rs_in,
    edge_out,
    edge_in,
    fin,
    halo_out,
    halo_in,
    load_sem,
    own_sem,
    a2a_send,
    a2a_recv,
    hr_send,
    hr_recv,
    ag_send,
    ag_recv,
    st_send,
    st_recv,
    rs_send,
    rs_recv,
    hg_send,
    hg_recv,
):
    Y, Z, H, G, NH, T = dims
    N = Y * Z
    d = lax.axis_index("ctx")
    hd = lax.axis_index("head")
    y = d // Z
    z = d % Z
    scaling = 1.0 / math.sqrt(HD)
    cexp = scaling * math.log2(math.e)

    d_next = (d + 1) % N
    d_prev = (d + N - 1) % N
    z_dev = lambda i: y * Z + i
    y_dev = lambda i: i * Z + z

    barrier = pltpu.get_barrier_semaphore()
    greet = [(z_dev((z + j) % Z), hd) for j in range(1, Z)]
    greet += [(y_dev((y + j) % Y), hd) for j in range(1, Y)]
    greet += [(d_next, hd), (d_prev, hd)]
    greet += [(d, (hd + j) % H) for j in range(1, H)]
    for dev in greet:
        pl.semaphore_signal(barrier, inc=1, device_id=dev, device_id_type=MESH)

    loads = [
        pltpu.make_async_copy(raw_hbm, raw_ref, load_sem.at[0]),
        pltpu.make_async_copy(taps_hbm, taps_ref, load_sem.at[1]),
        pltpu.make_async_copy(pos_hbm, pos_ref, load_sem.at[2]),
    ]
    for load in loads:
        load.start()

    def remote(src, dst, s_sem, r_sem, dev):
        return pltpu.make_async_remote_copy(
            src_ref=src, dst_ref=dst, send_sem=s_sem, recv_sem=r_sem, device_id=dev, device_id_type=MESH
        )

    tail_e = remote(
        raw_hbm.at[:, pl.ds(G - 16, 16)], halo_raw.at[0], hr_send.at[0], hr_recv.at[0], (d_next, hd)
    )
    tail_l = remote(
        raw_hbm.at[:, pl.ds(2 * G - 16, 16)], halo_raw.at[1], hr_send.at[1], hr_recv.at[1], (d_prev, hd)
    )
    RB = 2 * G // H
    CW = NH * HD

    def a2a(j):
        to = (hd + j) % H
        return remote(
            gout_ref.at[:, pl.ds(pl.multiple_of(to * CW, CW), CW)],
            land.at[pl.ds(pl.multiple_of(hd * RB, RB), RB)],
            a2a_send.at[j - 1],
            a2a_recv.at[j - 1],
            (d, to),
        )

    def a2a_in(j):
        frm = (hd + H - j) % H
        return remote(
            gout_ref.at[:, pl.ds(pl.multiple_of(hd * CW, CW), CW)],
            land.at[pl.ds(pl.multiple_of(frm * RB, RB), RB)],
            a2a_send.at[j - 1],
            a2a_recv.at[j - 1],
            (d, frm),
        )

    own = pltpu.make_async_copy(
        gout_ref.at[:, pl.ds(pl.multiple_of(hd * CW, CW), CW)],
        land.at[pl.ds(pl.multiple_of(hd * RB, RB), RB)],
        own_sem,
    )
    own.start()

    pl.semaphore_wait(barrier, len(greet))
    tail_e.start()
    tail_l.start()
    for j in range(1, H):
        a2a(j).start()
    for load in loads:
        load.wait()

    pair = pos_ref[0] // G
    rot = (pair - d + N) % N
    nk = Y * G
    nq = Z * G
    C = min(256, nq)
    group_of = lambda i: i >> (G.bit_length() - 1)

    def wrap(p):
        p = jnp.where(p >= 2 * N, p - 2 * N, p)
        return jnp.where(p >= N, p - N, p)

    def q_code(half, c):
        iq = lax.broadcasted_iota(jnp.int32, (1, C), 1) + c * C
        pq = wrap(group_of(iq) + (y * Z + rot))
        return pq * G + (iq & (G - 1)) if half == 0 else (iq & (G - 1)) - pq * G

    E = 16
    gathers = []
    for h in range(NH):
        gathers += [
            (lambda i, h=h: kv_all.at[0, h, :, i, pl.ds(E, G - E)], Y, y, y_dev),
            (lambda i, h=h: q_all.at[h, :, i, pl.ds(E, G - E)], Z, z, z_dev),
            (lambda i, h=h: kv_all.at[1, h, :, i, pl.ds(E, G - E)], Y, y, y_dev),
            (lambda i, h=h: d_all.at[h, :, i], Z, z, z_dev),
        ]
    gathers += [
        (lambda i: kv_all.at[:, :, :, i, pl.ds(0, E)], Y, y, y_dev),
        (lambda i: q_all.at[:, :, i, pl.ds(0, E)], Z, z, z_dev),
    ]
    K_EDGE, Q_EDGE = 4 * NH, 4 * NH + 1
    flips = [(h + f) % 2 for h in range(NH) for f in (0, 0, 1, 1)] + [0, 0]

    def steps_of(n, flip):
        a, b = n // 2, n - 1 - n // 2
        return (b, a) if flip else (a, b)

    def ag_copy(item, way, dist, incoming=False):
        view, n, me, dev_of = gathers[item]
        sign = 1 if way == 0 else n - 1
        near = dist <= 2 or item >= K_EDGE
        hop = dist if near else dist - 2
        if incoming:
            slot = (me + (n - sign) * dist) % n
        else:
            slot = me if near else (me + (n - sign) * 2) % n
        dev = (dev_of((me + sign * hop) % n), hd)
        return remote(
            view(slot), view(slot), ag_send.at[item, way, dist - 1], ag_recv.at[item, way, dist - 1], dev
        )

    def ag_counts(item):
        return enumerate(steps_of(gathers[item][1], flips[item]))

    def ag_first(item):
        for dist in (4, 3, 2, 1) if item >= K_EDGE else (2, 1):
            for way, count in ag_counts(item):
                if dist <= count:
                    ag_copy(item, way, dist).start()

    def ag_relay(item):
        for way, count in ag_counts(item):
            if count >= 2:
                ag_copy(item, way, 2, True).wait_recv()
            for dist in (4, 3):
                if dist <= count:
                    ag_copy(item, way, dist).start()

    def ag_last(item):
        for way, count in ag_counts(item):
            for dist in (1, 2, 3, 4) if item >= K_EDGE else (1, 3, 4):
                if dist <= count:
                    ag_copy(item, way, dist, True).wait_recv()

    zero_rows = jnp.zeros((16, CW), F32)

    def featurize(kind, half, prior, rows):
        x = raw_ref[kind, pl.ds(half * G, rows)].astype(F32)
        row = lax.broadcasted_iota(jnp.int32, (rows, CW), 0)
        tap = taps_ref[kind]
        out = tap[0:1] * x
        for t in range(1, T):
            moved = pltpu.roll(x, t, 0)
            if prior is not None:
                for i in range(t):
                    moved = jnp.where(row == i, prior[16 - t + i : 17 - t + i], moved)
            out = out + tap[t : t + 1] * moved
        return out.astype(BF16)

    def own_view(kind, h, half):
        return q_all.at[h, half, z] if kind == 0 else kv_all.at[kind - 1, h, half, y]

    for item, kind in enumerate((1, 0, 2)):
        for half in range(2):
            out = featurize(kind, half, None, G)
            for h in range(NH):
                own_view(kind, h, half)[pl.ds(E, G - E)] = out[E:, h * HD : (h + 1) * HD]
        for h in range(NH):
            ag_first(4 * h + item)

    tail_e.wait_recv()
    tail_l.wait_recv()
    for kind in range(3):
        for half in range(2):
            if half == 0:
                prior = jnp.where(pair == 0, zero_rows, halo_raw[0, kind].astype(F32))
            else:
                prior = jnp.where(
                    pair == N - 1, raw_ref[kind, pl.ds(G - 16, 16)].astype(F32), halo_raw[1, kind].astype(F32)
                )
            out = featurize(kind, half, prior, E)
            for h in range(NH):
                own_view(kind, h, half)[pl.ds(0, E)] = out[:, h * HD : (h + 1) * HD]
    ag_first(K_EDGE)
    ag_first(Q_EDGE)
    own.wait()
    for j in range(1, H):
        a2a_in(j).wait_recv()
    for half in range(2):
        for h in range(NH):
            d_all[h, half, z] = land[pl.ds(half * G, G), h * HD : (h + 1) * HD]
    for h in range(NH):
        ag_first(4 * h + 3)

    ik = lax.broadcasted_iota(jnp.int32, (nk, C), 0)
    pk = wrap(group_of(ik) * Z + (z + rot))
    k_code[0] = pk * G + (ik & (G - 1))
    k_code[1] = (ik & (G - 1)) - pk * G

    NT = (((1,), (1,)), ((), ()))
    TN = (((0,), (0,)), ((), ()))
    NN = (((1,), (0,)), ((), ()))

    def mm(a, b, how):
        return lax.dot_general(a, b, how, preferred_element_type=F32)

    zc = C // G
    lanes = C // 128

    def cols_of(half, c):
        return pl.ds(half * nq + c * C, C)

    def put_rows(ref, half, c, val):
        for i in range(lanes):
            ref[pl.ds((half * nq + c * C) // 128 + i, 1)] = val[:, i * 128 : (i + 1) * 128]

    def pass_score(h, half, c):
        q = q_all[h, half, pl.ds(c * zc, zc)].reshape(C, HD)
        score = []
        for kh in range(half + 1):
            sc = mm(kv_all[0, h, kh].reshape(nk, HD), q, NT)
            if kh == half:
                sc = jnp.where(k_code[half] <= q_code(half, c), sc, NEG)
            score.append(sc)
        top = jnp.max(score[0], axis=0, keepdims=True)
        if half == 1:
            top = jnp.maximum(top, jnp.max(score[1], axis=0, keepdims=True))
        total = jnp.zeros((1, C), F32)
        for kh in range(half + 1):
            w = jnp.exp2((score[kh] - top) * cexp)
            w_all[h, pl.ds(kh * nk, nk), cols_of(half, c)] = w
            total = total + jnp.sum(w, axis=0, keepdims=True)
        put_rows(stat_ml.at[h, z, 0], half, c, top)
        put_rows(stat_ml.at[h, z, 1], half, c, total)

    def pass_slope(h, half, c):
        g = d_all[h, half, pl.ds(c * zc, zc)].reshape(C, HD)
        tilt = jnp.zeros((1, C), F32)
        for kh in range(half + 1):
            slope = mm(kv_all[1, h, kh].reshape(nk, HD), g, NT)
            s_all[h, pl.ds(kh * nk, nk), cols_of(half, c)] = slope
            w = w_all[h, pl.ds(kh * nk, nk), cols_of(half, c)]
            tilt = tilt + jnp.sum(w * slope, axis=0, keepdims=True)
        put_rows(stat_t.at[h, z], half, c, tilt)

    def st_copy(which, h, j, incoming=False):
        slot = (z + Z - j) % Z if incoming else z
        dev = z_dev((z + Z - j) % Z if incoming else (z + j) % Z)
        ref = (stat_ml if which == 0 else stat_t).at[h, slot]
        return remote(ref, ref, st_send.at[which, h, j - 1], st_recv.at[which, h, j - 1], (dev, hd))

    def st_start(which, h):
        for j in sorted(range(1, Z), key=lambda j: -min(j, Z - j)):
            st_copy(which, h, j).start()

    def st_wait(which, h):
        for j in range(1, Z):
            st_copy(which, h, j, True).wait_recv()

    def st_finish_ml(h):
        st_wait(0, h)
        top = stat_ml[h, 0, 0]
        for i in range(1, Z):
            top = jnp.maximum(top, stat_ml[h, i, 0])
        total = jnp.zeros_like(top)
        rise = []
        for i in range(Z):
            rise.append(jnp.exp2((stat_ml[h, i, 0] - top) * cexp))
            total = total + stat_ml[h, i, 1] * rise[i]
        inv = 1.0 / total
        for i in range(Z):
            row_wt[h, i] = rise[i] * inv
        row_fac[h] = row_wt[h, z]

    def st_finish_t(h):
        st_wait(1, h)
        tilt = stat_t[h, 0] * row_wt[h, 0]
        for i in range(1, Z):
            tilt = tilt + stat_t[h, i] * row_wt[h, i]
        row_del[h] = tilt

    def row_of(ref, h, a, b):
        return jnp.concatenate([ref[h, pl.ds(i, 1)] for i in range(a // 128, b // 128)], axis=1)

    KC = min(256, nk)
    kz = KC // G

    def key_block(kh, c):
        lo = 0 if kh == 0 else nq
        return pl.ds(kh * nk + c * KC, KC), lo, pl.ds(lo, 2 * nq - lo)

    def of_queries(buf, h, kh):
        return buf[h].reshape(2 * nq, HD) if kh == 0 else buf[h, 1].reshape(nq, HD)

    def of_keys(kind, h, half):
        return kv_all[kind, h].reshape(2 * nk, HD) if half == 1 else kv_all[kind, h, 0].reshape(nk, HD)

    def pass_probs(h, kh, c):
        rows, lo, cols = key_block(kh, c)
        p = w_all[h, rows, cols] * row_of(row_fac, h, lo, 2 * nq)
        w_all[h, rows, cols] = p
        pb = p.astype(BF16)
        p_low[rows, cols] = pb
        part_y[1, h, kh, pl.ds(c * kz, kz)] = mm(pb, of_queries(d_all, h, kh), NN).reshape(kz, G, HD)

    def pass_out(h, half):
        p = p_low[pl.ds(0, nk * (half + 1)), pl.ds(half * nq, nq)]
        part_z[1, h, half] = mm(p, of_keys(1, h, half), TN).reshape(Z, G, HD)

    def pass_dscores(h, kh, c):
        rows, lo, cols = key_block(kh, c)
        x = w_all[h, rows, cols] * (s_all[h, rows, cols] - row_of(row_del, h, lo, 2 * nq))
        xb = x.astype(BF16)
        x_low[rows, cols] = xb
        part_y[0, h, kh, pl.ds(c * kz, kz)] = (mm(xb, of_queries(q_all, h, kh), NN) * scaling).reshape(kz, G, HD)

    def pass_dq(h, half):
        x = x_low[pl.ds(0, nk * (half + 1)), pl.ds(half * nq, nq)]
        part_z[0, h, half] = (mm(x, of_keys(0, h, half), TN) * scaling).reshape(Z, G, HD)

    def dq_like(which):
        return (part_z, Z, z, z_dev) if which == "z" else (part_y, Y, y, y_dev)

    O_ALL, Q_REST, K_REST, V_REST, DQ_EDGE, DK_EDGE, DV_EDGE = range(7)

    def sum_of(h, item):
        a, b = h % 2, (h + 1) % 2
        return (
            ("z", 1, 0, G, a),
            ("z", 0, E, G - E, a),
            ("y", 0, E, G - E, a),
            ("y", 1, E, G - E, a),
            ("z", 0, 0, E, b),
            ("y", 0, 0, E, b),
            ("y", 1, 0, E, b),
        )[item]

    def rs_bufs(h, item, way, dist):
        which, kind, row0, rows, flip = sum_of(h, item)
        if item >= DQ_EDGE:
            at = (h, item - DQ_EDGE, way, dist - 1)
            return edge_out.at[at], edge_in.at[at]
        at = (h, item, way, dist - 1, slice(None), pl.ds(row0, rows))
        return rs_out.at[at], rs_in.at[at]

    def rs_copy(h, item, way, dist):
        part, n, me, dev_of = dq_like(sum_of(h, item)[0])
        sign = 1 if way == 0 else n - 1
        hop = dist if dist <= 2 or item >= DQ_EDGE else dist - 2
        src, dst = rs_bufs(h, item, way, dist)
        return remote(
            src,
            dst,
            rs_send.at[h, item, way, dist - 1],
            rs_recv.at[h, item, way, dist - 1],
            (dev_of((me + sign * hop) % n), hd),
        )

    def rs_counts(h, item):
        which, kind, row0, rows, flip = sum_of(h, item)
        return enumerate(steps_of(Z if which == "z" else Y, flip))

    def rs_part(h, item, dest):
        which, kind, row0, rows, flip = sum_of(h, item)
        return dq_like(which)[0][kind, h, :, pl.ds(dest, 1), pl.ds(row0, rows)].reshape(2, rows, HD)

    def rs_put(h, item, way, dist):
        part, n, me, dev_of = dq_like(sum_of(h, item)[0])
        sign = 1 if way == 0 else n - 1
        val = rs_part(h, item, (me + sign * dist) % n)
        if dist == 2 and item < DQ_EDGE:
            count = steps_of(n, sum_of(h, item)[4])[way]
            for more in (3, 4):
                if more <= count:
                    rs_copy(h, item, way, more).wait_recv()
                    val = val + rs_bufs(h, item, way, more)[1][...].astype(F32)
        rs_bufs(h, item, way, dist)[0][...] = val.astype(BF16)
        rs_copy(h, item, way, dist).start()

    def rs_first(h, item):
        for dist in (4, 3, 2, 1) if item >= DQ_EDGE else (4, 3, 1):
            for way, count in rs_counts(h, item):
                if dist <= count:
                    rs_put(h, item, way, dist)

    def rs_relay(h, item):
        for way, count in rs_counts(h, item):
            if count >= 2:
                rs_put(h, item, way, 2)

    def rs_final(h, item):
        val = rs_part(h, item, z if sum_of(h, item)[0] == "z" else y)
        for way, count in rs_counts(h, item):
            for dist in (1, 2, 3, 4) if item >= DQ_EDGE else (1, 2):
                if dist <= count:
                    rs_copy(h, item, way, dist).wait_recv()
                    val = val + rs_bufs(h, item, way, dist)[1][...].astype(F32)
        return val

    def hg_copy(h, half):
        return remote(
            halo_out.at[h, half],
            halo_in.at[h, half],
            hg_send.at[h, half],
            hg_recv.at[h, half],
            (d_prev if half == 0 else d_next, hd),
        )

    def send_halo(h):
        for kind in range(3):
            for half in range(2):
                halo_out[h, half, kind] = fin[h, kind, half, 0:8]
        for half in range(2):
            hg_copy(h, half).start()

    def finish_edges(h):
        for kind, item in ((2, DV_EDGE), (1, DK_EDGE), (0, DQ_EDGE)):
            fin[h, kind, :, pl.ds(0, E)] = rs_final(h, item)

    def finish_sums(h, items):
        for item in items:
            val = rs_final(h, item)
            if item == O_ALL:
                for half in range(2):
                    attn_ref[pl.ds(half * G, G), h * HD : (h + 1) * HD] = val[half].astype(BF16)
            else:
                which, kind, row0, rows, flip = sum_of(h, item)
                fin[h, {Q_REST: 0, K_REST: 1, V_REST: 2}[item], :, pl.ds(row0, rows)] = val

    row1 = lax.broadcasted_iota(jnp.int32, (G, HD), 0)

    def wait_halo(h):
        for half in range(2):
            hg_copy(h, half).wait_recv()

    def finish_grads(h, kinds):
        for kind in kinds:
            tap = taps_ref[kind][:, h * HD : (h + 1) * HD]
            for half in range(2):
                x = fin[h, kind, half]
                if half == 0:
                    nxt = jnp.where(pair == N - 1, fin[h, kind, 1, 0:8], halo_in[h, 0, kind])
                else:
                    nxt = jnp.where(pair == 0, jnp.zeros((8, HD), F32), halo_in[h, 1, kind])
                out = tap[0:1] * x
                for t in range(1, T):
                    moved = pltpu.roll(x, G - t, 0)
                    for i in range(t):
                        moved = jnp.where(row1 == G - t + i, nxt[i : i + 1], moved)
                    out = out + tap[t : t + 1] * moved
                grad_ref[kind, pl.ds(half * G, G), h * HD : (h + 1) * HD] = out.astype(BF16)

    nc = nq // C
    kc = nk // KC
    chunks = [(1, c) for c in range(nc)] + [(0, c) for c in range(nc)]
    for item in (0, 1, 4, 5, 2, 6, 3, 7):
        ag_relay(item)
    for item in (0, 1, K_EDGE, Q_EDGE):
        ag_last(item)
    for half, c in chunks:
        pass_score(0, half, c)
    st_start(0, 0)
    ag_last(4)
    ag_last(5)
    for half, c in chunks:
        pass_score(1, half, c)
    st_start(0, 1)
    for h in range(NH):
        ag_last(4 * h + 2)
        ag_last(4 * h + 3)
        for half, c in chunks:
            pass_slope(h, half, c)
        st_start(1, h)
    for h in range(NH):
        st_finish_ml(h)
        for kh in range(2):
            for c in range(kc):
                pass_probs(h, kh, c)
        rs_first(h, DV_EDGE)
        rs_first(h, V_REST)
        for half in range(2):
            pass_out(h, half)
        rs_first(h, O_ALL)
    for h in range(NH):
        st_finish_t(h)
        for kh in range(2):
            for c in range(kc):
                pass_dscores(h, kh, c)
        rs_first(h, DK_EDGE)
        rs_first(h, K_REST)
        for half in range(2):
            pass_dq(h, half)
        rs_first(h, DQ_EDGE)
        rs_first(h, Q_REST)
    for h in range(NH):
        rs_relay(h, V_REST)
        rs_relay(h, O_ALL)
    for h in range(NH):
        rs_relay(h, K_REST)
        rs_relay(h, Q_REST)
    for h in range(NH):
        finish_edges(h)
        send_halo(h)
    for h in range(NH):
        finish_sums(h, (V_REST, O_ALL))
    for h in range(NH):
        wait_halo(h)
        finish_grads(h, (2,))
    for h in range(NH):
        finish_sums(h, (K_REST,))
        finish_grads(h, (1,))
        finish_sums(h, (Q_REST,))
        finish_grads(h, (0,))

    tail_e.wait_send()
    tail_l.wait_send()
    for j in range(1, H):
        a2a(j).wait_send()
    for item in range(len(gathers)):
        for way, count in ag_counts(item):
            for dist in range(1, count + 1):
                ag_copy(item, way, dist).wait_send()
    for h in range(NH):
        for item in range(7):
            for way, count in rs_counts(h, item):
                for dist in range(1, count + 1):
                    rs_copy(h, item, way, dist).wait_send()
        for j in range(1, Z):
            st_copy(0, h, j).wait_send()
            st_copy(1, h, j).wait_send()
        for half in range(2):
            hg_copy(h, half).wait_send()


def hand_on(attn_in, grad_in, attn_out, grad_out):
    attn_out[...] = attn_in[...]
    grad_out[...] = grad_in[...]


def local(Y, Z, H, qkv_raw, positions, filter_taps, grad_out):
    rows = positions.shape[0]
    G = rows // 2
    CW = qkv_raw.shape[2]
    NH = CW // HD
    T = filter_taps.shape[1]
    MR = max(Y, Z) // 2
    nq, nk = Z * G, Y * G
    C = min(256, nq)
    nr = 2 * nq // 128
    raw = jnp.transpose(qkv_raw, (1, 0, 2))
    dma = pltpu.SemaphoreType.DMA
    vmem = pl.BlockSpec(memory_space=pltpu.VMEM)
    attn, grad = pl.pallas_call(
        functools.partial(kernel, (Y, Z, H, G, NH, T)),
        out_shape=(
            jax.ShapeDtypeStruct((rows, CW), BF16),
            jax.ShapeDtypeStruct((3, rows, CW), BF16),
        ),
        in_specs=[pl.BlockSpec(memory_space=pltpu.HBM)] * 4,
        out_specs=(vmem, vmem),
        scratch_shapes=[
            pltpu.VMEM((3, rows, CW), BF16),
            pltpu.SMEM((rows,), jnp.int32),
            pltpu.VMEM(filter_taps.shape, F32),
            pltpu.VMEM((rows, CW), BF16),
            pltpu.VMEM((2, 3, 16, CW), BF16),
            pltpu.VMEM((NH, 2, Z, G, HD), BF16),
            pltpu.VMEM((NH, 2, Z, G, HD), BF16),
            pltpu.VMEM((2, NH, 2, Y, G, HD), BF16),
            pltpu.VMEM((2, nk, C), jnp.int32),
            pltpu.VMEM((NH, 2 * nk, 2 * nq), F32),
            pltpu.VMEM((NH, 2 * nk, 2 * nq), F32),
            pltpu.VMEM((2 * nk, 2 * nq), BF16),
            pltpu.VMEM((2 * nk, 2 * nq), BF16),
            pltpu.VMEM((NH, Z, 2, nr, 128), F32),
            pltpu.VMEM((NH, Z, nr, 128), F32),
            pltpu.VMEM((NH, Z, nr, 128), F32),
            pltpu.VMEM((NH, nr, 128), F32),
            pltpu.VMEM((NH, nr, 128), F32),
            pltpu.VMEM((2, NH, 2, Z, G, HD), F32),
            pltpu.VMEM((2, NH, 2, Y, G, HD), F32),
            pltpu.VMEM((NH, 4, 2, MR, 2, G, HD), BF16),
            pltpu.VMEM((NH, 4, 2, MR, 2, G, HD), BF16),
            pltpu.VMEM((NH, 3, 2, MR, 2, 16, HD), BF16),
            pltpu.VMEM((NH, 3, 2, MR, 2, 16, HD), BF16),
            pltpu.VMEM((NH, 3, 2, G, HD), F32),
            pltpu.VMEM((NH, 2, 3, 8, HD), F32),
            pltpu.VMEM((NH, 2, 3, 8, HD), F32),
            dma((3,)),
            dma,
            dma((H - 1,)),
            dma((H - 1,)),
            dma((2,)),
            dma((2,)),
            dma((4 * NH + 2, 2, MR)),
            dma((4 * NH + 2, 2, MR)),
            dma((2, NH, Z - 1)),
            dma((2, NH, Z - 1)),
            dma((NH, 7, 2, MR)),
            dma((NH, 7, 2, MR)),
            dma((NH, 2)),
            dma((NH, 2)),
        ],
        compiler_params=pltpu.CompilerParams(
            collective_id=0, has_side_effects=True, vmem_limit_bytes=56 * 1024 * 1024
        ),
    )(raw, positions, filter_taps, grad_out)
    attn, grad = pl.pallas_call(
        hand_on,
        out_shape=(
            jax.ShapeDtypeStruct((rows, CW), BF16),
            jax.ShapeDtypeStruct((3, rows, CW), BF16),
        ),
        in_specs=[vmem, vmem],
        out_specs=(vmem, vmem),
    )(attn, grad)
    return attn, jnp.transpose(grad, (1, 0, 2))


def solution(mesh):
    n = mesh.shape["ctx"]
    Y = 1
    while (2 * Y) * (2 * Y) <= n and n % (2 * Y) == 0:
        Y *= 2
    in_specs = (P("ctx", None, "head"), P("ctx"), P(None, None, "head"), P(("ctx", "head"), None))
    out_specs = (P("ctx", "head"), P("ctx", None, "head"))
    return jax.shard_map(
        functools.partial(local, Y, n // Y, mesh.shape["head"]),
        mesh=mesh,
        in_specs=in_specs,
        out_specs=out_specs,
        check_vma=False,
    )
```
